128 devices in a mesh: gz: 32 (over z, y, x_lo), gy: 4 (over x_hi, core).
Axes of the slice: x: 4 (x_hi: 2, x_lo: 2; x = x_hi * 2 + x_lo), y: 4, z: 4, core: 2. Of those that a mesh axis runs over, the one named last changes fastest.
Arguments:
- fields: bfloat16 [64, 128, 128, 128], P('gz', 'gy'), may hold values from -6 to 6
- cotangent: bfloat16 [64, 128, 128, 128], P('gz', 'gy'), may hold values from -6 to 6
- w_value: bfloat16 [128, 128], replicated, may hold values from -0.5 to 0.5
- w_out: bfloat16 [128, 128], replicated, may hold values from -0.5 to 0.5
- w_query: float32 [3, 128, 128], replicated, may hold values from -5 to 5
- w_key: float32 [3, 128, 128], replicated, may hold values from -5 to 5
Outputs:
- field_grad: bfloat16 [64, 128, 128, 128], P('gz', 'gy')
- value_grad: float32 [128, 128], replicated
- output_grad: float32 [128, 128], replicated
- query_grad: float32 [3, 128, 128], replicated
- key_grad: float32 [3, 128, 128], replicated
The draws below stay inside these ranges and needn't reach their ends.
All inputs are finite; a program needn't handle non-finite values.
Results may differ from the reference program's by a relative error of at most 0.0095.
Values may be sent and summed in bfloat16 or wider, within the bound.
A program may use at most 128 MiB of HBM per device.

```python
import math
import jax
import jax.numpy as jnp
from jax import lax

C = 128
H = 8
NX = 128
NZ = 64
NY = 128


def shared_parts(key):
    head_scale = jax.random.uniform(jax.random.fold_in(key, 5), (3, H), jnp.float32, 0.0, 1.0)
    return head_scale


def projection(key, head_scale, strength_top):
    own = jax.random.truncated_normal(key, -4.0, 4.0, (3, C, C), jnp.float32)
    strengths = jnp.exp(head_scale * math.log(strength_top))
    column_scale = jnp.repeat(strengths, C // H, axis=1)[:, None, :]
    return own * column_scale / math.sqrt(C)


def draw_w_query(key, part):
    head_scale = shared_parts(key)
    key = jax.random.fold_in(key, 11)
    return projection(key, head_scale, 1.0)


def draw_w_key(key, part):
    head_scale = shared_parts(key)
    key = jax.random.fold_in(key, 12)
    return projection(key, head_scale, 1.0)


def shard_levels(key, shape, cuts, least, high):
    gain, own = 1.0, jax.random.fold_in(key, 6)
    for dim, parts in cuts:
        heights = jnp.exp(jax.random.uniform(jax.random.fold_in(own, dim), (parts,), jnp.float32, least / len(cuts), high / len(cuts)))
        gain = gain * jnp.repeat(heights, shape[dim] // parts).reshape([-1 if axis == dim else 1 for axis in range(len(shape))])
    return gain


def gaussian(key, extent, spread, most, cuts=(), held_as=jnp.bfloat16):
    values = jax.random.normal(key, extent, jnp.float32) * spread
    if len(cuts) > 0:
        values = shard_levels(key, extent, cuts, -0.22, 0.18) * values
    return jnp.clip(values, min=-most, max=most).astype(held_as)


def setup_inputs(seed: int = 0) -> dict:
    streams_of = jax.random.split(jax.random.key(seed), 7)
    return {
        "fields": gaussian(streams_of[0], (NZ, NY, NX, C), 1.0, 6.0, ((0, 32), (1, 4))),
        "cotangent": gaussian(streams_of[1], (NZ, NY, NX, C), 1.0, 6.0, ((0, 32), (1, 4))),
        "w_value": gaussian(streams_of[2], (C, C), C ** -0.5, 0.5),
        "w_out": gaussian(streams_of[3], (C, C), C ** -0.5, 0.5),
        "w_query": draw_w_query(jax.random.fold_in(streams_of[6], 71), 0),
        "w_key": draw_w_key(jax.random.fold_in(streams_of[6], 71), 0),
    }


epsilon = 1e-06

def attend_one(pooled, query_weight, key_weight):
    channels = pooled.shape[-1]
    head_size = channels // H
    length = pooled.shape[0]
    mean_square = lax.optimization_barrier(jnp.mean(pooled * pooled, axis=-1, keepdims=True))
    normed = pooled * lax.rsqrt(mean_square + epsilon)
    queries = jnp.dot(normed, query_weight, precision=lax.Precision.HIGHEST).reshape(length, H, head_size)
    keys_all = jnp.dot(normed, key_weight, precision=lax.Precision.HIGHEST).reshape(length, H, head_size)
    scores = jnp.einsum('ihd,jhd->hij', queries, keys_all, precision=lax.Precision.HIGHEST) / math.sqrt(head_size)
    return jax.nn.softmax(scores, axis=-1)

def attend_all(means_z, means_y, means_x, w_query, w_key):
    return (attend_one(means_z, w_query[0], w_key[0]), attend_one(means_y, w_query[1], w_key[1]), attend_one(means_x, w_query[2], w_key[2]))

def apply_axis(field, matrix, axis):
    matrix_wide = matrix.astype(jnp.float32)
    if axis == 2:
        return lax.map(lambda section: jnp.einsum('hij,yjhd->yihd', matrix_wide, section.astype(jnp.float32)).astype(jnp.bfloat16), field)
    if axis == 1:
        return lax.map(lambda section: jnp.einsum('hij,jxhd->ixhd', matrix_wide, section.astype(jnp.float32)).astype(jnp.bfloat16), field)
    turned = jnp.swapaxes(field, 0, 1)
    finished = lax.map(lambda section: jnp.einsum('hij,jxhd->ixhd', matrix_wide, section.astype(jnp.float32)).astype(jnp.bfloat16), turned)
    return jnp.swapaxes(finished, 0, 1)

def pair_sum(left_side, right_side, axis):
    length = left_side.shape[axis]
    if axis == 0:
        left_side = jnp.swapaxes(left_side, 0, 1)
        right_side = jnp.swapaxes(right_side, 0, 1)
        pattern = 'ixhd,jxhd->hij'
    elif axis == 1:
        pattern = 'ixhd,jxhd->hij'
    else:
        pattern = 'yihd,yjhd->hij'

    def accumulate(carry, pieces):
        return (carry + jnp.einsum(pattern, pieces[0].astype(jnp.float32), pieces[1].astype(jnp.float32)), None)
    start_sum = jnp.zeros((H, length, length), jnp.float32)
    result, unused = lax.scan(accumulate, start_sum, (left_side, right_side))
    return result

def reference(fields, cotangent, w_value, w_out, w_query, w_key):
    head_size = C // H
    flat_fields = fields.reshape(NZ * NY * NX, C)
    values = jnp.dot(flat_fields, w_value, preferred_element_type=jnp.float32).astype(jnp.bfloat16).reshape(NZ, NY, NX, H, head_size)
    means_z = lax.optimization_barrier(jnp.sum(fields, axis=(1, 2), dtype=jnp.float32)) / (NY * NX)
    means_y = lax.optimization_barrier(jnp.sum(fields, axis=(0, 2), dtype=jnp.float32)) / (NZ * NX)
    means_x = lax.optimization_barrier(jnp.sum(fields, axis=(0, 1), dtype=jnp.float32)) / (NZ * NY)
    attn_z, attn_y, attn_x = attend_all(means_z, means_y, means_x, w_query, w_key)
    kernel_z = attn_z.astype(jnp.bfloat16)
    kernel_y = attn_y.astype(jnp.bfloat16)
    kernel_x = attn_x.astype(jnp.bfloat16)
    after_x = apply_axis(values, kernel_x, 2)
    after_y = apply_axis(after_x, kernel_y, 1)
    mixed = apply_axis(after_y, kernel_z, 0)
    flat_cot = cotangent.reshape(NZ * NY * NX, C)
    output_grad = jnp.dot(mixed.reshape(NZ * NY * NX, C).T, flat_cot, preferred_element_type=jnp.float32)
    grad_mixed = jnp.dot(flat_cot, w_out.T, preferred_element_type=jnp.float32).astype(jnp.bfloat16).reshape(NZ, NY, NX, H, head_size)
    score_z = pair_sum(grad_mixed, after_y, 0)
    grad_y = apply_axis(grad_mixed, jnp.swapaxes(kernel_z, 1, 2), 0)
    score_y = pair_sum(grad_y, after_x, 1)
    grad_x = apply_axis(grad_y, jnp.swapaxes(kernel_y, 1, 2), 1)
    score_x = pair_sum(grad_x, values, 2)
    grad_values = apply_axis(grad_x, jnp.swapaxes(kernel_x, 1, 2), 2)
    flat_grad = grad_values.reshape(NZ * NY * NX, C)
    value_grad = jnp.dot(flat_fields.T, flat_grad, preferred_element_type=jnp.float32)
    unused, pull = jax.vjp(attend_all, means_z, means_y, means_x, w_query, w_key)
    dmean_z, dmean_y, dmean_x, query_grad, key_grad = pull((score_z, score_y, score_x))
    direct = jnp.dot(flat_grad, w_value.T, preferred_element_type=jnp.float32).reshape(NZ, NY, NX, C)
    field_grad = (direct + dmean_z[:, None, None, :] / (NY * NX) + dmean_y[None, :, None, :] / (NZ * NX) + dmean_x[None, None, :, :] / (NZ * NY)).astype(jnp.bfloat16)
    return (field_grad, value_grad, output_grad, query_grad, key_grad)
```

```python
import functools

import jax
import jax.numpy as jnp
from jax import lax
from jax.experimental import pallas as pl
from jax.experimental.pallas import tpu as pltpu
from jax.sharding import PartitionSpec as P

BF = jnp.bfloat16
F32 = jnp.float32
MESH = pl.DeviceIdType.MESH
H = 8
D = 16
C = 128
Z, Y, X = 64, 128, 128
ZL, YL = 2, 32
CELLS = ZL * YL
GZ, GY = 32, 4
EPS = 1e-06
HIGH = lax.Precision.HIGHEST
COUNTS = (Y * X, Z * X, Z * Y)
STARTS = (0, Z, Z + Y)
LENGTHS = (Z, Y, X)
POOLED = Z + Y + X
VMEM = pl.BlockSpec(memory_space=pltpu.VMEM)


def params(**more):
    return pltpu.CompilerParams(vmem_limit_bytes=56 * 2**20, **more)


def dot(a, b):
    return jnp.dot(a, b, preferred_element_type=F32)


def dot_nt(a, b, precision=None):
    return lax.dot_general(
        a, b, (((1,), (1,)), ((), ())), preferred_element_type=F32, precision=precision
    )


def dot_tn(a, b, precision=None):
    return lax.dot_general(
        a, b, (((0,), (0,)), ((), ())), preferred_element_type=F32, precision=precision
    )


def head_stack(block):
    head = lax.broadcasted_iota(jnp.int32, block.shape, 1) % C // D
    zero = jnp.zeros((), block.dtype)
    return jnp.concatenate([jnp.where(head == h, block, zero) for h in range(H)], axis=0)


def pair_lanes(first, second):
    return jnp.concatenate([first, second], axis=1)


def turn_kernel(src, dst):
    dst[...] = jnp.swapaxes(src[...], 0, 1)


def turn(field):
    return pl.pallas_call(
        turn_kernel,
        grid=(4,),
        in_specs=[pl.BlockSpec((16, X, C), lambda i: (i, 0, 0))],
        out_specs=pl.BlockSpec((X, 16, C), lambda i: (0, i, 0)),
        out_shape=jax.ShapeDtypeStruct((X, CELLS, C), BF),
        compiler_params=params(),
    )(field)


def sums_kernel(src, out):
    step = pl.program_id(0)

    @pl.when(step == 0)
    def clear():
        out[...] = jnp.zeros_like(out)

    block = src[...].astype(F32)
    cells = jnp.sum(block, axis=1)
    gz, gy = lax.axis_index("gz"), lax.axis_index("gy")
    out[pl.ds(Z + Y, X), :] += jnp.sum(block, axis=0)
    out[pl.ds(gz * ZL + step // 2, 1), :] += jnp.sum(cells, axis=0, keepdims=True)
    y_start = pl.multiple_of(Z + gy * YL + (step % 2) * 16, 16)
    out[pl.ds(y_start, 16), :] += cells


def sums(fields):
    return pl.pallas_call(
        sums_kernel,
        grid=(4,),
        in_specs=[pl.BlockSpec((16, X, C), lambda i: (i, 0, 0))],
        out_specs=pl.BlockSpec((POOLED, C), lambda i: (0, 0)),
        out_shape=jax.ShapeDtypeStruct((POOLED, C), F32),
        compiler_params=params(),
    )(fields)


def after_kernel(src, w_value, kernel_x, dst, held):
    values = dot(src[...].reshape(16 * X, C), w_value[...]).astype(BF).reshape(16, X, C)
    for t in range(0, 16, 2):
        wide = head_stack(pair_lanes(values[t], values[t + 1]))
        done = dot(kernel_x[...], wide).astype(BF)
        held[t] = done[:, :C]
        held[t + 1] = done[:, C:]
    dst[...] = jnp.swapaxes(held[...], 0, 1)


def after_all(fields, w_value, kernel_x):
    return pl.pallas_call(
        after_kernel,
        grid=(4,),
        in_specs=[
            pl.BlockSpec((16, X, C), lambda i: (i, 0, 0)),
            pl.BlockSpec((C, C), lambda i: (0, 0)),
            pl.BlockSpec((X, H * X), lambda i: (0, 0)),
        ],
        out_specs=pl.BlockSpec((X, 16, C), lambda i: (0, i, 0)),
        out_shape=jax.ShapeDtypeStruct((X, CELLS, C), BF),
        scratch_shapes=[pltpu.VMEM((16, X, C), BF)],
        compiler_params=params(),
    )(fields, w_value, kernel_x)


def home_kernel(grad, src, w_value, back_x, grad_values, score_x, value_grad):
    @pl.when(pl.program_id(0) == 0)
    def clear():
        score_x[...] = jnp.zeros_like(score_x)
        value_grad[...] = jnp.zeros_like(value_grad)

    grad_x = jnp.swapaxes(grad[...], 0, 1)
    flat = src[...].reshape(16 * X, C)
    values = dot(flat, w_value[...]).astype(BF).reshape(16, X, C)
    total = jnp.zeros((H * X, X), F32)
    for t in range(0, 16, 2):
        wide = head_stack(pair_lanes(grad_x[t], grad_x[t + 1]))
        done = dot(back_x[...], wide).astype(BF)
        grad_values[t] = done[:, :C]
        grad_values[t + 1] = done[:, C:]
        total += dot_nt(wide, pair_lanes(values[t], values[t + 1]))
    score_x[...] += total
    value_grad[...] += dot_tn(flat, grad_values[...].reshape(16 * X, C))


def home(grad, fields, w_value, back_x):
    return pl.pallas_call(
        home_kernel,
        grid=(4,),
        in_specs=[
            pl.BlockSpec((X, 16, C), lambda i: (0, i, 0)),
            pl.BlockSpec((16, X, C), lambda i: (i, 0, 0)),
            pl.BlockSpec((C, C), lambda i: (0, 0)),
            pl.BlockSpec((X, H * X), lambda i: (0, 0)),
        ],
        out_specs=[
            pl.BlockSpec((16, X, C), lambda i: (i, 0, 0)),
            pl.BlockSpec((H * X, X), lambda i: (0, 0)),
            pl.BlockSpec((C, C), lambda i: (0, 0)),
        ],
        out_shape=[
            jax.ShapeDtypeStruct((CELLS, X, C), BF),
            jax.ShapeDtypeStruct((H * X, X), F32),
            jax.ShapeDtypeStruct((C, C), F32),
        ],
        compiler_params=params(),
    )(grad, fields, w_value, back_x)


def finish_kernel(grad_values, w_value, means_grad, out):
    step = pl.program_id(0)
    gz, gy = lax.axis_index("gz"), lax.axis_index("gy")
    direct = dot_nt(grad_values[...].reshape(16 * X, C), w_value[...]).reshape(16, X, C)
    part_z = means_grad[pl.ds(gz * ZL + step // 2, 1), :] / COUNTS[0]
    y_start = pl.multiple_of(Z + gy * YL + (step % 2) * 16, 16)
    part_y = means_grad[pl.ds(y_start, 16), :] / COUNTS[1]
    part_x = means_grad[pl.ds(Z + Y, X), :] / COUNTS[2]
    cells = part_z + part_y
    out[...] = (direct + cells[:, None, :] + part_x[None]).astype(BF)


def finish(grad_values, w_value, means_grad):
    return pl.pallas_call(
        finish_kernel,
        grid=(4,),
        in_specs=[
            pl.BlockSpec((16, X, C), lambda i: (i, 0, 0)),
            pl.BlockSpec((C, C), lambda i: (0, 0)),
            pl.BlockSpec((POOLED, C), lambda i: (0, 0)),
        ],
        out_specs=pl.BlockSpec((16, X, C), lambda i: (i, 0, 0)),
        out_shape=jax.ShapeDtypeStruct((CELLS, X, C), BF),
        compiler_params=params(),
    )(grad_values, w_value, means_grad)


def far_back_kernel(cot, w_out, back_z, back_y, cot_y, mixed_y, grad_y, grad_out, held):
    def over_z(step, carry):
        side, start = step // 2, pl.multiple_of((step % 2) * 16, 16)
        block = cot[:, side, :, pl.ds(start, 16), :].reshape(Z, 16, C)
        turned = jnp.swapaxes(block, 0, 1)
        y_start = pl.multiple_of(step * 16, 16)
        cot_y[pl.ds(y_start, 16)] = turned
        grad_mixed = dot_nt(turned.reshape(16 * Z, C), w_out[...]).astype(BF).reshape(16, Z, C)
        mixed_y[pl.ds(y_start, 16)] = grad_mixed
        for t in range(0, 16, 2):
            wide = head_stack(pair_lanes(grad_mixed[t], grad_mixed[t + 1]))
            done = dot(back_z[...], wide).astype(BF)
            held[t] = done[:, :C]
            held[t + 1] = done[:, C:]
        grad_y[:, pl.ds(y_start, 16), :] = jnp.swapaxes(held[...], 0, 1)
        return carry

    lax.fori_loop(0, 8, over_z, 0)

    def over_y(t, carry):
        wide = head_stack(pair_lanes(grad_y[2 * t], grad_y[2 * t + 1]))
        done = dot(back_y[...], wide).astype(BF)
        for side in range(GY):
            for low in range(ZL):
                grad_out[t, side, low] = done[side * YL : (side + 1) * YL, low * C : (low + 1) * C]
        return carry

    lax.fori_loop(0, Z // 2, over_y, 0)


def far_back(cot, w_out, back_z, back_y):
    return pl.pallas_call(
        far_back_kernel,
        in_specs=[VMEM] * 4,
        out_specs=[VMEM] * 4,
        out_shape=[
            jax.ShapeDtypeStruct((Y, Z, C), BF),
            jax.ShapeDtypeStruct((Y, Z, C), BF),
            jax.ShapeDtypeStruct((Z, Y, C), BF),
            jax.ShapeDtypeStruct((GZ, GY, ZL, YL, C), BF),
        ],
        scratch_shapes=[pltpu.VMEM((16, Z, C), BF)],
        compiler_params=params(),
        cost_estimate=pl.CostEstimate(flops=3 * 10**9, bytes_accessed=10 * 2**20, transcendentals=0),
    )(cot, w_out, back_z, back_y)


def far_kernel(after, cot_y, mixed_y, grad_y, kernel_z, kernel_y, score_z, score_y, out_grad, held):
    score_z[...] = jnp.zeros_like(score_z)
    score_y[...] = jnp.zeros_like(score_y)
    out_grad[...] = jnp.zeros_like(out_grad)

    def over_y(t, carry):
        lines = [after[t, :, low].reshape(Y, C) for low in range(ZL)]
        block = pair_lanes(lines[0], lines[1])
        done = dot(kernel_y[...], head_stack(block)).astype(BF)
        held[2 * t] = done[:, :C]
        held[2 * t + 1] = done[:, C:]
        score_y[...] += dot_nt(head_stack(pair_lanes(grad_y[2 * t], grad_y[2 * t + 1])), block)
        return carry

    lax.fori_loop(0, Z // 2, over_y, 0)

    def over_z(step, carry):
        y_start = pl.multiple_of(step * 16, 16)
        after_y = jnp.swapaxes(held[:, pl.ds(y_start, 16), :], 0, 1)
        grad_mixed = mixed_y[pl.ds(y_start, 16)]
        parts = []
        total = jnp.zeros((H * Z, Z), F32)
        for t in range(0, 16, 2):
            block = pair_lanes(after_y[t], after_y[t + 1])
            done = dot(kernel_z[...], head_stack(block)).astype(BF)
            parts += [done[:, :C], done[:, C:]]
            total += dot_nt(head_stack(pair_lanes(grad_mixed[t], grad_mixed[t + 1])), block)
        score_z[...] += total
        mixed = jnp.concatenate(parts, axis=0)
        out_grad[...] += dot_tn(mixed, cot_y[pl.ds(y_start, 16)].reshape(16 * Z, C))
        return carry

    lax.fori_loop(0, 8, over_z, 0)


def far(after, cot_y, mixed_y, grad_y, kernel_z, kernel_y):
    return pl.pallas_call(
        far_kernel,
        in_specs=[VMEM] * 6,
        out_specs=[VMEM] * 3,
        out_shape=[
            jax.ShapeDtypeStruct((H * Z, Z), F32),
            jax.ShapeDtypeStruct((H * Y, Y), F32),
            jax.ShapeDtypeStruct((C, C), F32),
        ],
        scratch_shapes=[pltpu.VMEM((Z, Y, C), BF)],
        compiler_params=params(),
        cost_estimate=pl.CostEstimate(flops=6 * 10**9, bytes_accessed=10 * 2**20, transcendentals=0),
    )(after, cot_y, mixed_y, grad_y, kernel_z, kernel_y)


def normalise(pooled, axis):
    means = pooled[pl.ds(STARTS[axis], LENGTHS[axis]), :] / COUNTS[axis]
    scale = lax.rsqrt(jnp.mean(means * means, axis=-1, keepdims=True) + EPS)
    return means * scale, scale


def project(normed, weight):
    return jnp.dot(normed, weight, preferred_element_type=F32, precision=HIGH)


def maps_kernel(pooled, w_query, w_key, *outs):
    for axis in range(3):
        length = LENGTHS[axis]
        attn, kernel, back = outs[3 * axis : 3 * axis + 3]
        normed, _ = normalise(pooled, axis)
        queries = project(normed, w_query[axis])
        keys = project(normed, w_key[axis])
        scores = dot_nt(head_stack(queries), keys, HIGH) * (1.0 / D**0.5)
        grown = jnp.exp(scores - jnp.max(scores, axis=-1, keepdims=True))
        soft = grown / jnp.sum(grown, axis=-1, keepdims=True)
        attn[...] = soft
        heads = [soft[h * length : (h + 1) * length] for h in range(H)]
        kernel[...] = jnp.concatenate(heads, axis=1).astype(BF)
        back[...] = jnp.concatenate([head.T for head in heads], axis=1).astype(BF)


def maps(pooled, w_query, w_key):
    shapes = []
    for length in LENGTHS:
        shapes += [
            jax.ShapeDtypeStruct((H * length, length), F32),
            jax.ShapeDtypeStruct((length, H * length), BF),
            jax.ShapeDtypeStruct((length, H * length), BF),
        ]
    return pl.pallas_call(
        maps_kernel,
        in_specs=[VMEM] * 3,
        out_specs=[VMEM] * 9,
        out_shape=shapes,
        compiler_params=params(),
    )(pooled, w_query, w_key)


def pull_kernel(pooled, w_query, w_key, attn_z, attn_y, attn_x, score_z, score_y, score_x, value_grad, out_grad, out):
    for axis, (attn, score) in enumerate(((attn_z, score_z), (attn_y, score_y), (attn_x, score_x))):
        length, start = LENGTHS[axis], STARTS[axis]
        normed, _ = normalise(pooled, axis)
        queries = head_stack(project(normed, w_query[axis]))
        keys = head_stack(project(normed, w_key[axis]))
        soft, grad = attn[...], score[...]
        inner = jnp.sum(soft * grad, axis=-1, keepdims=True)
        grad = soft * (grad - inner) * (1.0 / D**0.5)
        heads = [grad[h * length : (h + 1) * length] for h in range(H)]
        out[pl.ds(start, length), :] = jnp.dot(
            jnp.concatenate(heads, axis=1), keys, preferred_element_type=F32, precision=HIGH
        )
        out[pl.ds(POOLED + start, length), :] = dot_tn(grad, queries, HIGH)
    out[pl.ds(2 * POOLED, C), :] = value_grad[...]
    out[pl.ds(2 * POOLED + C, C), :] = out_grad[...]


def pull(pooled, w_query, w_key, attns, scores, value_grad, out_grad):
    return pl.pallas_call(
        pull_kernel,
        in_specs=[VMEM] * 11,
        out_specs=VMEM,
        out_shape=jax.ShapeDtypeStruct((2 * POOLED + 2 * C, C), F32),
        compiler_params=params(),
    )(pooled, w_query, w_key, *attns, *scores, value_grad, out_grad)


def settle_kernel(pooled, w_query, w_key, total, means_grad, query_grad, key_grad, value_grad, out_grad):
    for axis in range(3):
        length, start = LENGTHS[axis], STARTS[axis]
        normed, scale = normalise(pooled, axis)
        grad_q = total[pl.ds(start, length), :]
        grad_k = total[pl.ds(POOLED + start, length), :]
        query_grad[axis] = dot_tn(normed, grad_q, HIGH)
        key_grad[axis] = dot_tn(normed, grad_k, HIGH)
        grad = dot_nt(grad_q, w_query[axis], HIGH) + dot_nt(grad_k, w_key[axis], HIGH)
        inner = jnp.mean(grad * normed, axis=-1, keepdims=True)
        means_grad[pl.ds(start, length), :] = scale * (grad - normed * inner)
    value_grad[...] = total[pl.ds(2 * POOLED, C), :]
    out_grad[...] = total[pl.ds(2 * POOLED + C, C), :]


def settle(pooled, w_query, w_key, total):
    return pl.pallas_call(
        settle_kernel,
        in_specs=[VMEM] * 4,
        out_specs=[VMEM] * 5,
        out_shape=[
            jax.ShapeDtypeStruct((POOLED, C), F32),
            jax.ShapeDtypeStruct((3, C, C), F32),
            jax.ShapeDtypeStruct((3, C, C), F32),
            jax.ShapeDtypeStruct((C, C), F32),
            jax.ShapeDtypeStruct((C, C), F32),
        ],
        compiler_params=params(),
    )(pooled, w_query, w_key, total)


def sum_kernel(src, out, near, wide, near_send, near_recv, wide_send, wide_recv, back_send, back_recv):
    gz, gy = lax.axis_index("gz"), lax.axis_index("gy")
    line, side = gz // 2, (gz % 2) * 4 + gy
    piece = src.shape[0] // 8

    def near_peer(k):
        peer = (side + k) % 8
        return peer, (line * 2 + peer // 4, peer % 4)

    def wide_peer(k):
        peer = (line + k) % 16
        return peer, (peer * 2 + gz % 2, gy)

    barrier = pltpu.get_barrier_semaphore()
    for k in range(1, 8):
        pl.semaphore_signal(barrier, inc=1, device_id=near_peer(k)[1], device_id_type=MESH)
    for k in range(1, 16):
        pl.semaphore_signal(barrier, inc=1, device_id=wide_peer(k)[1], device_id_type=MESH)
    pl.semaphore_wait(barrier, 22)

    def rows(index):
        return pl.ds(pl.multiple_of(index * piece, 8), piece)

    for k in range(1, 8):
        peer, device = near_peer(k)
        pltpu.make_async_remote_copy(
            src.at[rows(peer)], near.at[side], near_send, near_recv, device_id=device, device_id_type=MESH
        ).start()
    near[side] = src[rows(side)]
    sent = near.at[pl.ds(0, 7)]
    pltpu.make_async_copy(sent, sent, near_recv).wait()
    wide[line] = jnp.sum(near[...], axis=0)
    for k in range(1, 16):
        peer, device = wide_peer(k)
        pltpu.make_async_remote_copy(
            wide.at[line], wide.at[line], wide_send, wide_recv, device_id=device, device_id_type=MESH
        ).start()
    sent_wide = wide.at[pl.ds(0, 15)]
    pltpu.make_async_copy(sent_wide, sent_wide, wide_recv).wait()
    out[rows(side)] = jnp.sum(wide[...], axis=0)
    for k in range(1, 8):
        peer, device = near_peer(k)
        pltpu.make_async_remote_copy(
            out.at[rows(side)], out.at[rows(side)], back_send, back_recv, device_id=device, device_id_type=MESH
        ).start()
    pltpu.make_async_copy(sent, sent, back_recv).wait()
    pltpu.make_async_copy(sent, sent, near_send).wait()
    pltpu.make_async_copy(sent_wide, sent_wide, wide_send).wait()
    pltpu.make_async_copy(sent, sent, back_send).wait()


def sum_all(parts, collective_id):
    rows = parts.shape[0]
    return pl.pallas_call(
        sum_kernel,
        in_specs=[VMEM],
        out_specs=VMEM,
        out_shape=jax.ShapeDtypeStruct(parts.shape, F32),
        scratch_shapes=[
            pltpu.VMEM((8, rows // 8, C), F32),
            pltpu.VMEM((16, rows // 8, C), F32),
        ]
        + [pltpu.SemaphoreType.DMA] * 6,
        compiler_params=params(collective_id=collective_id, has_side_effects=True),
    )(parts)


def exchange(blocks):
    return lax.all_to_all(blocks, ("gz", "gy"), split_axis=0, concat_axis=0, tiled=True)


def local(fields, cotangent, w_value, w_out, w_query, w_key):
    fields = fields.reshape(CELLS, X, C)
    far_cot = exchange(turn(cotangent.reshape(CELLS, X, C))).reshape(GZ, GY, ZL, YL, C)
    pooled = sum_all(sums(fields), 0)
    attn_z, kernel_z, back_z, attn_y, kernel_y, back_y, attn_x, kernel_x, back_x = maps(
        pooled, w_query, w_key
    )
    after = exchange(after_all(fields, w_value, kernel_x)).reshape(GZ, GY, ZL, YL, C)
    cot_y, mixed_y, grad_y, grad_out = far_back(far_cot, w_out, back_z, back_y)
    grad_home = exchange(grad_out.reshape(X, CELLS, C))
    score_z, score_y, out_part = far(after, cot_y, mixed_y, grad_y, kernel_z, kernel_y)
    grad_values, score_x, value_part = home(grad_home, fields, w_value, back_x)
    total = sum_all(
        pull(
            pooled, w_query, w_key, (attn_z, attn_y, attn_x), (score_z, score_y, score_x), value_part, out_part
        ),
        1,
    )
    means_grad, query_grad, key_grad, value_grad, out_grad = settle(pooled, w_query, w_key, total)
    field_grad = finish(grad_values, w_value, means_grad).reshape(ZL, YL, X, C)
    return (field_grad, value_grad, out_grad, query_grad, key_grad)


def solution(mesh):
    placed = (P("gz", "gy", None, None), P("gz", "gy", None, None), P(), P(), P(), P())
    return jax.shard_map(
        local,
        mesh=mesh,
        in_specs=placed,
        out_specs=(P("gz", "gy", None, None), P(), P(), P(), P()),
        check_vma=False,
    )
```

```python
import jax
import jax.numpy as jnp
from jax import lax
from jax.experimental import pallas as pl
from jax.experimental.pallas import tpu as pltpu
from jax.sharding import PartitionSpec as P

BF = jnp.bfloat16
F32 = jnp.float32
MESH = pl.DeviceIdType.MESH
H = 8
D = 16
C = 128
Z, Y, X = 64, 128, 128
ZL, YL = 2, 32
CELLS = ZL * YL
GZ, GY = 32, 4
EPS = 1e-06
HIGH = lax.Precision.HIGHEST
COUNTS = (Y * X, Z * X, Z * Y)
STARTS = (0, Z, Z + Y)
LENGTHS = (Z, Y, X)
POOLED = Z + Y + X
VMEM = pl.BlockSpec(memory_space=pltpu.VMEM)


def params(**more):
    return pltpu.CompilerParams(vmem_limit_bytes=56 * 2**20, **more)


def dot(a, b):
    return jnp.dot(a, b, preferred_element_type=F32)


def dot_nt(a, b, precision=None):
    return lax.dot_general(
        a, b, (((1,), (1,)), ((), ())), preferred_element_type=F32, precision=precision
    )


def dot_tn(a, b, precision=None):
    return lax.dot_general(
        a, b, (((0,), (0,)), ((), ())), preferred_element_type=F32, precision=precision
    )


def head_stack(block):
    head = lax.broadcasted_iota(jnp.int32, block.shape, 1) % C // D
    zero = jnp.zeros((), block.dtype)
    return jnp.concatenate([jnp.where(head == h, block, zero) for h in range(H)], axis=0)


def pair_lanes(first, second):
    return jnp.concatenate([first, second], axis=1)


def normalise(pooled, axis):
    means = pooled[pl.ds(STARTS[axis], LENGTHS[axis]), :] / COUNTS[axis]
    scale = lax.rsqrt(jnp.mean(means * means, axis=-1, keepdims=True) + EPS)
    return means * scale, scale


def project(normed, weight):
    return jnp.dot(normed, weight, preferred_element_type=F32, precision=HIGH)


def attention(pooled, w_query, w_key, axis, attn, kernel, back):
    length = LENGTHS[axis]
    normed, _ = normalise(pooled, axis)
    queries = project(normed, w_query[axis])
    keys = project(normed, w_key[axis])
    scores = dot_nt(head_stack(queries), keys, HIGH) * (1.0 / D**0.5)
    grown = jnp.exp(scores - jnp.max(scores, axis=-1, keepdims=True))
    soft = grown / jnp.sum(grown, axis=-1, keepdims=True)
    attn[...] = soft
    heads = [soft[h * length : (h + 1) * length] for h in range(H)]
    kernel[...] = jnp.concatenate(heads, axis=1).astype(BF)
    back[...] = jnp.concatenate([head.T for head in heads], axis=1).astype(BF)


def pull(pooled, w_query, w_key, axis, attn, score, out, row_q, row_k):
    length = LENGTHS[axis]
    normed, _ = normalise(pooled, axis)
    queries = head_stack(project(normed, w_query[axis]))
    keys = head_stack(project(normed, w_key[axis]))
    soft, grad = attn[...], score[...]
    inner = jnp.sum(soft * grad, axis=-1, keepdims=True)
    grad = soft * (grad - inner) * (1.0 / D**0.5)
    heads = [grad[h * length : (h + 1) * length] for h in range(H)]
    out[pl.ds(row_q, length), :] = jnp.dot(
        jnp.concatenate(heads, axis=1), keys, preferred_element_type=F32, precision=HIGH
    )
    out[pl.ds(row_k, length), :] = dot_tn(grad, queries, HIGH)


def settle(pooled, w_query, w_key, axis, total, row_q, row_k, query_grad, key_grad):
    length = LENGTHS[axis]
    normed, scale = normalise(pooled, axis)
    grad_q = total[pl.ds(row_q, length), :]
    grad_k = total[pl.ds(row_k, length), :]
    query_grad[axis] = dot_tn(normed, grad_q, HIGH)
    key_grad[axis] = dot_tn(normed, grad_k, HIGH)
    grad = dot_nt(grad_q, w_query[axis], HIGH) + dot_nt(grad_k, w_key[axis], HIGH)
    inner = jnp.mean(grad * normed, axis=-1, keepdims=True)
    return scale * (grad - normed * inner) / COUNTS[axis]


def place():
    gz, gy = lax.axis_index("gz"), lax.axis_index("gy")
    return gz // 8, (gz // 2) % 4, (gy // 2) * 2 + gz % 2, gy % 2


def shifted(step):
    z, y, x, core = place()
    k = (step * 37) % 128
    to_core = (core + k) % 2
    to_x = (x + (k // 2)) % 4
    to_y = (y + (k // 8)) % 4
    to_z = (z + (k // 32)) % 4
    return (to_z * 4 + to_y) * 2 + to_x % 2, (to_x // 2) * 2 + to_core


def mine():
    return lax.axis_index("gz") * GY + lax.axis_index("gy")


def wait_bytes(ref, sem):
    pltpu.make_async_copy(ref, ref, sem).wait()


def send_all(src, dst, send_sem, recv_sem):
    me = mine()

    def send(step, carry):
        gz, gy = shifted(step)
        pltpu.make_async_remote_copy(
            src.at[gz * GY + gy], dst.at[me], send_sem, recv_sem, device_id=(gz, gy), device_id_type=MESH
        ).start()
        return carry

    lax.fori_loop(1, 128, send, 0)
    dst[me] = src[me]


def wait_all(ref, sem):
    wait_bytes(ref.at[pl.ds(0, 127)], sem)


class Sum:
    def __init__(self, src, out, near, wide, sems):
        self.src, self.out, self.near, self.wide, self.sems = src, out, near, wide, sems
        self.piece = src.shape[0] // 8
        gz, gy = lax.axis_index("gz"), lax.axis_index("gy")
        self.gz, self.gy = gz, gy
        self.line, self.side = gz // 2, (gz % 2) * 4 + gy

    def rows(self, index):
        return pl.ds(pl.multiple_of(index * self.piece, 8), self.piece)

    def near_peer(self, k):
        peer = (self.side + k) % 8
        return peer, (self.line * 2 + peer // 4, peer % 4)

    def wide_peer(self, k):
        peer = (self.line + k) % 16
        return peer, (peer * 2 + self.gz % 2, self.gy)

    def copy(self, src, dst, first, device):
        pltpu.make_async_remote_copy(
            src, dst, self.sems.at[first], self.sems.at[first + 1], device_id=device, device_id_type=MESH
        ).start()

    def first(self):
        for k in range(1, 8):
            peer, device = self.near_peer(k)
            self.copy(self.src.at[self.rows(peer)], self.near.at[self.side], 0, device)
        self.near[self.side] = self.src[self.rows(self.side)]

    def second(self):
        wait_bytes(self.near.at[pl.ds(0, 7)], self.sems.at[1])
        self.wide[self.line] = jnp.sum(self.near[...], axis=0)
        for k in range(1, 16):
            peer, device = self.wide_peer(k)
            self.copy(self.wide.at[self.line], self.wide.at[self.line], 2, device)

    def third(self):
        wait_bytes(self.wide.at[pl.ds(0, 15)], self.sems.at[3])
        rows = self.rows(self.side)
        self.out[rows] = jnp.sum(self.wide[...], axis=0)
        for k in range(1, 8):
            peer, device = self.near_peer(k)
            self.copy(self.out.at[rows], self.out.at[rows], 4, device)

    def end(self):
        wait_bytes(self.near.at[pl.ds(0, 7)], self.sems.at[5])

    def close(self):
        wait_bytes(self.near.at[pl.ds(0, 7)], self.sems.at[0])
        wait_bytes(self.wide.at[pl.ds(0, 15)], self.sems.at[2])
        wait_bytes(self.near.at[pl.ds(0, 7)], self.sems.at[4])


def whole_kernel(
    fields_in, cot_in, w_value, w_out, w_query, w_key,
    field_grad, value_grad, out_grad, query_grad, key_grad,
    fields, cot, cot_s, cot_r, cot_y, mixed_y, grad_y, grad_s, after_s, after_r, after_y, grad_r, values, grad_values, direct,
    held,
    attn_z, kernel_z, back_z, attn_y, kernel_y, back_y, attn_x, kernel_x, back_x,
    score_z, score_y, score_x, value_part,
    sum0, pooled, near0, wide0, sum1, total1, near1, wide1, sum2, total2, near2, wide2,
    load_sems, store_sems, move_sems, sums0, sums1, sums2,
):
    gz, gy = lax.axis_index("gz"), lax.axis_index("gy")

    def load(i, src, dst, base):
        return pltpu.make_async_copy(src.at[pl.ds(16 * i, 16)], dst.at[pl.ds(16 * i, 16)], load_sems.at[base + i])

    for i in range(4):
        load(i, fields_in, fields, 0).start()
    for i in range(4):
        load(i, cot_in, cot, 4).start()

    barrier = pltpu.get_barrier_semaphore()

    def greet(step, carry):
        pl.semaphore_signal(barrier, inc=1, device_id=shifted(step), device_id_type=MESH)
        return carry

    lax.fori_loop(1, 128, greet, 0)

    sum0[...] = jnp.zeros_like(sum0)
    for i in range(4):
        load(i, fields_in, fields, 0).wait()
        block = fields[pl.ds(16 * i, 16)].astype(F32)
        cells = jnp.sum(block, axis=1)
        sum0[pl.ds(Z + Y, X), :] += jnp.sum(block, axis=0)
        sum0[pl.ds(gz * ZL + i // 2, 1), :] += jnp.sum(cells, axis=0, keepdims=True)
        sum0[pl.ds(pl.multiple_of(Z + gy * YL + (i % 2) * 16, 16), 16), :] += cells
    means = Sum(sum0, pooled, near0, wide0, sums0)
    pl.semaphore_wait(barrier, 127)
    means.first()
    for i in range(4):
        load(i, cot_in, cot, 4).wait()
        cot_s[:, pl.ds(16 * i, 16), :] = jnp.swapaxes(cot[pl.ds(16 * i, 16)], 0, 1)
    means.second()
    for i in range(4):
        flat = fields[pl.ds(16 * i, 16)].reshape(16 * X, C)
        values[pl.ds(16 * i, 16)] = dot(flat, w_value[...]).astype(BF).reshape(16, X, C)
    means.third()
    send_all(cot_s, cot_r, move_sems.at[0], move_sems.at[1])
    means.end()

    attention(pooled, w_query, w_key, 2, attn_x, kernel_x, back_x)
    means.close()

    def over_x(i, carry):
        start = pl.multiple_of(i * 16, 16)
        for t in range(0, 16, 2):
            wide = head_stack(pair_lanes(values[start + t], values[start + t + 1]))
            done = dot(kernel_x[...], wide).astype(BF)
            held[t] = done[:, :C]
            held[t + 1] = done[:, C:]
        after_s[:, pl.ds(start, 16), :] = jnp.swapaxes(held[...], 0, 1)
        return carry

    lax.fori_loop(0, 4, over_x, 0)
    send_all(after_s, after_r, move_sems.at[2], move_sems.at[3])
    attention(pooled, w_query, w_key, 0, attn_z, kernel_z, back_z)
    attention(pooled, w_query, w_key, 1, attn_y, kernel_y, back_y)

    wait_all(cot_r, move_sems.at[1])

    def back_over_z(step, carry):
        side, start = step // 2, pl.multiple_of((step % 2) * 16, 16)
        y_start = pl.multiple_of(step * 16, 16)
        lines = []
        for low in range(ZL):
            lines.append(
                jnp.stack(
                    [cot_r[g * GY + side, pl.ds(low * YL + start, 16), :] for g in range(GZ)], axis=0
                )
            )
        block = jnp.stack(lines, axis=1).reshape(Z, 16, C)
        turned = jnp.swapaxes(block, 0, 1)
        cot_y[pl.ds(y_start, 16)] = turned
        grad_mixed = dot_nt(turned.reshape(16 * Z, C), w_out[...]).astype(BF).reshape(16, Z, C)
        mixed_y[pl.ds(y_start, 16)] = grad_mixed
        for t in range(0, 16, 2):
            wide = head_stack(pair_lanes(grad_mixed[t], grad_mixed[t + 1]))
            done = dot(back_z[...], wide).astype(BF)
            held[t, pl.ds(0, Z), :] = done[:, :C]
            held[t + 1, pl.ds(0, Z), :] = done[:, C:]
        grad_y[:, pl.ds(y_start, 16), :] = jnp.swapaxes(held[:, pl.ds(0, Z), :], 0, 1)
        return carry

    lax.fori_loop(0, 8, back_over_z, 0)

    def back_over_y(t, carry):
        wide = head_stack(pair_lanes(grad_y[2 * t], grad_y[2 * t + 1]))
        done = dot(back_y[...], wide).astype(BF)
        for side in range(GY):
            for low in range(ZL):
                grad_s[t * GY + side, pl.ds(low * YL, YL), :] = done[
                    side * YL : (side + 1) * YL, low * C : (low + 1) * C
                ]
        return carry

    lax.fori_loop(0, Z // 2, back_over_y, 0)
    send_all(grad_s, grad_r, move_sems.at[4], move_sems.at[5])

    score_z[...] = jnp.zeros_like(score_z)
    score_y[...] = jnp.zeros_like(score_y)
    sum1[pl.ds(2 * (Z + Y), C), :] = jnp.zeros((C, C), F32)
    wait_all(after_r, move_sems.at[3])

    def over_y(t, carry):
        lines = []
        for low in range(ZL):
            lines.append(
                jnp.concatenate([after_r[t * GY + side, pl.ds(low * YL, YL), :] for side in range(GY)], axis=0)
            )
        block = pair_lanes(lines[0], lines[1])
        done = dot(kernel_y[...], head_stack(block)).astype(BF)
        after_y[2 * t] = done[:, :C]
        after_y[2 * t + 1] = done[:, C:]
        score_y[...] += dot_nt(head_stack(pair_lanes(grad_y[2 * t], grad_y[2 * t + 1])), block)
        return carry

    lax.fori_loop(0, Z // 2, over_y, 0)

    def over_z(step, carry):
        y_start = pl.multiple_of(step * 16, 16)
        lines = jnp.swapaxes(after_y[:, pl.ds(y_start, 16), :], 0, 1)
        grad_mixed = mixed_y[pl.ds(y_start, 16)]
        parts = []
        total = jnp.zeros((H * Z, Z), F32)
        for t in range(0, 16, 2):
            block = pair_lanes(lines[t], lines[t + 1])
            done = dot(kernel_z[...], head_stack(block)).astype(BF)
            parts += [done[:, :C], done[:, C:]]
            total += dot_nt(head_stack(pair_lanes(grad_mixed[t], grad_mixed[t + 1])), block)
        score_z[...] += total
        mixed = jnp.concatenate(parts, axis=0)
        sum1[pl.ds(2 * (Z + Y), C), :] += dot_tn(mixed, cot_y[pl.ds(y_start, 16)].reshape(16 * Z, C))
        return carry

    lax.fori_loop(0, 8, over_z, 0)
    pull(pooled, w_query, w_key, 0, attn_z, score_z, sum1, 0, Z)
    pull(pooled, w_query, w_key, 1, attn_y, score_y, sum1, 2 * Z, 2 * Z + Y)
    early = Sum(sum1, total1, near1, wide1, sums1)
    early.first()

    score_x[...] = jnp.zeros_like(score_x)
    value_part[...] = jnp.zeros_like(value_part)
    wait_all(grad_r, move_sems.at[5])

    def home(i, carry):
        start = pl.multiple_of(i * 16, 16)
        grad_x = jnp.swapaxes(grad_r[:, pl.ds(start, 16), :], 0, 1)
        total = jnp.zeros((H * X, X), F32)
        for t in range(0, 16, 2):
            wide = head_stack(pair_lanes(grad_x[t], grad_x[t + 1]))
            done = dot(back_x[...], wide).astype(BF)
            grad_values[start + t] = done[:, :C]
            grad_values[start + t + 1] = done[:, C:]
            total += dot_nt(wide, pair_lanes(values[start + t], values[start + t + 1]))
        score_x[...] += total
        grad = grad_values[pl.ds(start, 16)].reshape(16 * X, C)
        value_part[...] += dot_tn(fields[pl.ds(start, 16)].reshape(16 * X, C), grad)
        return carry

    lax.fori_loop(0, 2, home, 0)
    early.second()
    lax.fori_loop(2, 4, home, 0)
    early.third()
    pull(pooled, w_query, w_key, 2, attn_x, score_x, sum2, 0, X)
    sum2[pl.ds(2 * X, C), :] = value_part[...]
    late = Sum(sum2, total2, near2, wide2, sums2)
    late.first()
    early.end()
    means_z = settle(pooled, w_query, w_key, 0, total1, 0, Z, query_grad, key_grad)
    late.second()
    means_y = settle(pooled, w_query, w_key, 1, total1, 2 * Z, 2 * Z + Y, query_grad, key_grad)
    out_grad[...] = total1[pl.ds(2 * (Z + Y), C), :]
    sum0[pl.ds(0, Z), :] = means_z
    sum0[pl.ds(Z, Y), :] = means_y
    late.third()

    def project_back(i, carry):
        start = pl.multiple_of(i * 16, 16)
        grad = grad_values[pl.ds(start, 16)].reshape(16 * X, C)
        direct[pl.ds(start, 16)] = dot_nt(grad, w_value[...]).reshape(16, X, C)
        return carry

    lax.fori_loop(0, 4, project_back, 0)
    late.end()
    means_x = settle(pooled, w_query, w_key, 2, total2, 0, X, query_grad, key_grad)
    value_grad[...] = total2[pl.ds(2 * X, C), :]

    def store(i):
        return pltpu.make_async_copy(grad_values.at[pl.ds(16 * i, 16)], field_grad.at[pl.ds(16 * i, 16)], store_sems.at[i])

    for i in range(4):
        part_z = sum0[pl.ds(gz * ZL + i // 2, 1), :]
        part_y = sum0[pl.ds(pl.multiple_of(Z + gy * YL + (i % 2) * 16, 16), 16), :]
        cells = part_z + part_y
        grad_values[pl.ds(16 * i, 16)] = (direct[pl.ds(16 * i, 16)] + cells[:, None, :] + means_x[None]).astype(BF)
        store(i).start()
    for i in range(4):
        store(i).wait()
    wait_all(cot_s, move_sems.at[0])
    wait_all(after_s, move_sems.at[2])
    wait_all(grad_s, move_sems.at[4])
    early.close()
    late.close()


def local(fields, cotangent, w_value, w_out, w_query, w_key):
    any_space = pl.BlockSpec(memory_space=pl.ANY)
    cells = (CELLS, X, C)
    blocks = (X, CELLS, C)
    sums = []
    for rows in (POOLED, 2 * (Z + Y) + C, 2 * X + C):
        sums += [
            pltpu.VMEM((rows, C), F32),
            pltpu.VMEM((rows, C), F32),
            pltpu.VMEM((8, rows // 8, C), F32),
            pltpu.VMEM((16, rows // 8, C), F32),
        ]
    map_shapes = []
    for length in LENGTHS:
        map_shapes += [
            pltpu.VMEM((H * length, length), F32),
            pltpu.VMEM((length, H * length), BF),
            pltpu.VMEM((length, H * length), BF),
        ]
    field_shapes = [
        cells, cells, blocks, blocks, (Y, Z, C), (Y, Z, C), (Z, Y, C), blocks, blocks, blocks, (Z, Y, C), blocks,
        cells, cells,
    ]
    square = jax.ShapeDtypeStruct((C, C), F32)
    cube = jax.ShapeDtypeStruct((3, C, C), F32)
    field_grad, value_grad, out_grad, query_grad, key_grad = pl.pallas_call(
        whole_kernel,
        in_specs=[any_space] * 2 + [VMEM] * 4,
        out_specs=[any_space] + [VMEM] * 4,
        out_shape=[jax.ShapeDtypeStruct(cells, BF), square, square, cube, cube],
        scratch_shapes=[pltpu.VMEM(shape, BF) for shape in field_shapes]
        + [pltpu.VMEM(cells, F32), pltpu.VMEM((16, X, C), BF)]
        + map_shapes
        + [
            pltpu.VMEM((H * Z, Z), F32),
            pltpu.VMEM((H * Y, Y), F32),
            pltpu.VMEM((H * X, X), F32),
            pltpu.VMEM((C, C), F32),
        ]
        + sums
        + [pltpu.SemaphoreType.DMA((count,)) for count in (8, 4, 6, 6, 6, 6)],
        compiler_params=params(collective_id=0, has_side_effects=True),
    )(fields.reshape(cells), cotangent.reshape(cells), w_value, w_out, w_query, w_key)
    return (field_grad.reshape(ZL, YL, X, C), value_grad, out_grad, query_grad, key_grad)


def solution(mesh):
    placed = (P("gz", "gy", None, None), P("gz", "gy", None, None), P(), P(), P(), P())
    return jax.shard_map(
        local,
        mesh=mesh,
        in_specs=placed,
        out_specs=(P("gz", "gy", None, None), P(), P(), P(), P()),
        check_vma=False,
    )
```

```python
import jax
import jax.numpy as jnp
from jax import lax
from jax.experimental import pallas as pl
from jax.experimental.pallas import tpu as pltpu
from jax.sharding import PartitionSpec as P

BF = jnp.bfloat16
F32 = jnp.float32
MESH = pl.DeviceIdType.MESH
H = 8
D = 16
C = 128
Z, Y, X = 64, 128, 128
ZL, YL = 2, 32
CELLS = ZL * YL
GZ, GY = 32, 4
EPS = 1e-06
HIGH = lax.Precision.HIGHEST
COUNTS = (Y * X, Z * X, Z * Y)
STARTS = (0, Z, Z + Y)
LENGTHS = (Z, Y, X)
POOLED = Z + Y + X
VMEM = pl.BlockSpec(memory_space=pltpu.VMEM)


def params(**more):
    return pltpu.CompilerParams(vmem_limit_bytes=56 * 2**20, **more)


def dot(a, b):
    return jnp.dot(a, b, preferred_element_type=F32)


def dot_nt(a, b, precision=None):
    return lax.dot_general(
        a, b, (((1,), (1,)), ((), ())), preferred_element_type=F32, precision=precision
    )


def dot_tn(a, b, precision=None):
    return lax.dot_general(
        a, b, (((0,), (0,)), ((), ())), preferred_element_type=F32, precision=precision
    )


def head_stack(block):
    head = lax.broadcasted_iota(jnp.int32, block.shape, 1) % C // D
    zero = jnp.zeros((), block.dtype)
    return jnp.concatenate([jnp.where(head == h, block, zero) for h in range(H)], axis=0)


def mix(kernel, lines):
    done = dot(kernel[...], head_stack(jnp.concatenate(lines, axis=1))).astype(BF)
    return [done[:, C * t : C * (t + 1)] for t in range(len(lines))]


def pair_up(left, right):
    return dot_nt(head_stack(jnp.concatenate(left, axis=1)), jnp.concatenate(right, axis=1))


def normalise(pooled, axis):
    means = pooled[pl.ds(STARTS[axis], LENGTHS[axis]), :] / COUNTS[axis]
    scale = lax.rsqrt(jnp.mean(means * means, axis=-1, keepdims=True) + EPS)
    return means * scale, scale


def project(normed, weight):
    return jnp.dot(normed, weight, preferred_element_type=F32, precision=HIGH)


def attention(pooled, w_query, w_key, axis, attn, kernel, back):
    length = LENGTHS[axis]
    normed, _ = normalise(pooled, axis)
    queries = project(normed, w_query[axis])
    keys = project(normed, w_key[axis])
    scores = dot_nt(head_stack(queries), keys, HIGH) * (1.0 / D**0.5)
    grown = jnp.exp(scores - jnp.max(scores, axis=-1, keepdims=True))
    soft = grown / jnp.sum(grown, axis=-1, keepdims=True)
    attn[...] = soft
    heads = [soft[h * length : (h + 1) * length] for h in range(H)]
    kernel[...] = jnp.concatenate(heads, axis=1).astype(BF)
    back[...] = jnp.concatenate([head.T for head in heads], axis=1).astype(BF)


def pull(pooled, w_query, w_key, axis, attn, score, out, row_q, row_k):
    length = LENGTHS[axis]
    normed, _ = normalise(pooled, axis)
    queries = head_stack(project(normed, w_query[axis]))
    keys = head_stack(project(normed, w_key[axis]))
    soft, grad = attn[...], score[...]
    inner = jnp.sum(soft * grad, axis=-1, keepdims=True)
    grad = soft * (grad - inner) * (1.0 / D**0.5)
    heads = [grad[h * length : (h + 1) * length] for h in range(H)]
    out[pl.ds(row_q, length), :] = jnp.dot(
        jnp.concatenate(heads, axis=1), keys, preferred_element_type=F32, precision=HIGH
    )
    out[pl.ds(row_k, length), :] = dot_tn(grad, queries, HIGH)


def settle(pooled, w_query, w_key, axis, total, row_q, row_k, out, out_q, out_k):
    length = LENGTHS[axis]
    normed, scale = normalise(pooled, axis)
    grad_q = total[pl.ds(row_q, length), :]
    grad_k = total[pl.ds(row_k, length), :]
    out[pl.ds(out_q, C), :] = dot_tn(normed, grad_q, HIGH)
    out[pl.ds(out_k, C), :] = dot_tn(normed, grad_k, HIGH)
    grad = dot_nt(grad_q, w_query[axis], HIGH) + dot_nt(grad_k, w_key[axis], HIGH)
    inner = jnp.mean(grad * normed, axis=-1, keepdims=True)
    return scale * (grad - normed * inner) / COUNTS[axis]


def torus():
    gz, gy = lax.axis_index("gz"), lax.axis_index("gy")
    z, y = lax.div(gz, 8), lax.rem(lax.div(gz, 2), 4)
    x, core = lax.div(gy, 2) * 2 + lax.rem(gz, 2), lax.rem(gy, 2)
    lines = [
        [(lax.rem(z + dz, 4) * 4 + lax.rem(y + dy, 4)) * 2 for dy in range(4)] for dz in range(4)
    ]
    return lines, x, core


def shifts(step, first=0):
    lines, x, core = torus()
    to_core = lax.rem(core + lax.rem(step, 2), 2)
    turn = x + lax.div(step, 2)
    sides = []
    for dx in range(4):
        to_x = lax.rem(turn + dx, 4)
        sides.append((lax.rem(to_x, 2), lax.div(to_x, 2) * 2 + to_core))
    found = []
    for j in range(first, 16):
        dz, dy = j % 4, (j // 4 + j) % 4
        low, gy = sides[(j // 4 + 2 * j) % 4]
        found.append((lines[dz][dy] + low, gy))
    return found


def each_device(visit, first, last):
    def step(i, carry):
        for device in shifts(i):
            visit(device)
        return carry

    if first == 0:
        for device in shifts(jnp.int32(0), 1):
            visit(device)
        first = 1
    lax.fori_loop(first, last, step, 0)


def mine():
    return lax.axis_index("gz") * GY + lax.axis_index("gy")


def wait_bytes(ref, sem):
    pltpu.make_async_copy(ref, ref, sem).wait()


def send(src, dst, send_sem, recv_sem, first=0, last=8, part=None):
    me = mine()

    def block(ref, index):
        return ref.at[index] if part is None else ref.at[index, part]

    def visit(device):
        pltpu.make_async_remote_copy(
            block(src, device[0] * GY + device[1]), block(dst, me), send_sem, recv_sem,
            device_id=device, device_id_type=MESH,
        ).start()

    each_device(visit, first, last)


def keep(src, dst):
    me = mine()
    dst[me] = src[me]


def wait_all(ref, sem, part=None):
    if part is None:
        wait_bytes(ref.at[pl.ds(0, 127)], sem)
    else:
        wait_bytes(ref.at[pl.ds(0, 127), part], sem)


class Sum:
    def __init__(self, src, out, near, wide, sems):
        self.src, self.out, self.near, self.wide, self.sems = src, out, near, wide, sems
        self.piece = src.shape[0] // 8
        gz, gy = lax.axis_index("gz"), lax.axis_index("gy")
        self.gz, self.gy = gz, gy
        self.line, self.side = lax.div(gz, 2), lax.rem(gz, 2) * 4 + gy

    def rows(self, index):
        return pl.ds(pl.multiple_of(index * self.piece, 8), self.piece)

    def near_peer(self, k):
        peer = lax.rem(self.side + k, 8)
        return peer, (self.line * 2 + lax.div(peer, 4), lax.rem(peer, 4))

    def wide_peer(self, k):
        peer = lax.rem(self.line + k, 16)
        return peer, (peer * 2 + lax.rem(self.gz, 2), self.gy)

    def copy(self, src, dst, first, device):
        pltpu.make_async_remote_copy(
            src, dst, self.sems.at[first], self.sems.at[first + 1], device_id=device, device_id_type=MESH
        ).start()

    def first(self):
        for k in range(1, 8):
            peer, device = self.near_peer(k)
            self.copy(self.src.at[self.rows(peer)], self.near.at[self.side], 0, device)
        self.near[self.side] = self.src[self.rows(self.side)]

    def second(self):
        wait_bytes(self.near.at[pl.ds(0, 7)], self.sems.at[1])
        self.wide[self.line] = jnp.sum(self.near[...], axis=0)
        for k in range(1, 16):
            peer, device = self.wide_peer(k)
            self.copy(self.wide.at[self.line], self.wide.at[self.line], 2, device)

    def third(self):
        wait_bytes(self.wide.at[pl.ds(0, 15)], self.sems.at[3])
        rows = self.rows(self.side)
        self.out[rows] = jnp.sum(self.wide[...], axis=0)
        for k in range(1, 8):
            peer, device = self.near_peer(k)
            self.copy(self.out.at[rows], self.out.at[rows], 4, device)

    def end(self):
        wait_bytes(self.near.at[pl.ds(0, 7)], self.sems.at[5])

    def close(self):
        wait_bytes(self.near.at[pl.ds(0, 7)], self.sems.at[0])
        wait_bytes(self.wide.at[pl.ds(0, 15)], self.sems.at[2])
        wait_bytes(self.near.at[pl.ds(0, 7)], self.sems.at[4])


def whole_kernel(
    fields_in, cot_in, w_value_in, w_out_in, w_query_in, w_key_in,
    grad_values_out, rest_out,
    fields, cot, cot_s, cot_r, cot_y, mixed_y, grad_y, grad_s, after_s, after_r, after_y, grad_r, values, grad_values,
    held, w_value, w_out, w_query, w_key,
    attn_z, kernel_z, back_z, attn_y, kernel_y, back_y, attn_x, kernel_x, back_x,
    score_z, score_y, score_x, early_rest,
    sum0, pooled, near0, wide0, sum1, total1, near1, wide1, sum2, total2, near2, wide2,
    load_sems, store_sems, move_sems, sums0, sums1, sums2,
):
    gz, gy = lax.axis_index("gz"), lax.axis_index("gy")

    def load(i, src, dst, base):
        return pltpu.make_async_copy(src.at[pl.ds(16 * i, 16)], dst.at[pl.ds(16 * i, 16)], load_sems.at[base + i])

    weights = [
        pltpu.make_async_copy(src, dst, load_sems.at[8 + i])
        for i, (src, dst) in enumerate(
            ((w_value_in, w_value), (w_out_in, w_out), (w_query_in, w_query), (w_key_in, w_key))
        )
    ]
    for i in range(4):
        load(i, fields_in, fields, 0).start()
    for i in range(4):
        load(i, cot_in, cot, 4).start()
    for copy in weights:
        copy.start()

    barrier = pltpu.get_barrier_semaphore()

    def greet(device):
        pl.semaphore_signal(barrier, inc=1, device_id=device, device_id_type=MESH)

    each_device(greet, 0, 8)

    sum0[...] = jnp.zeros_like(sum0)
    for i in range(4):
        load(i, fields_in, fields, 0).wait()
        block = fields[pl.ds(16 * i, 16)].astype(F32)
        cells = jnp.sum(block, axis=1)
        sum0[pl.ds(Z + Y, X), :] += jnp.sum(block, axis=0)
        sum0[pl.ds(gz * ZL + i // 2, 1), :] += jnp.sum(cells, axis=0, keepdims=True)
        sum0[pl.ds(pl.multiple_of(Z + gy * YL + (i % 2) * 16, 16), 16), :] += cells
    means = Sum(sum0, pooled, near0, wide0, sums0)
    for i in range(4):
        load(i, cot_in, cot, 4).wait()
        cot_s[:, pl.ds(16 * i, 16), :] = jnp.swapaxes(cot[pl.ds(16 * i, 16)], 0, 1)
    for copy in weights:
        copy.wait()
    pl.semaphore_wait(barrier, 127)
    means.first()
    send(cot_s, cot_r, move_sems.at[0], move_sems.at[1], 0, 2)
    keep(cot_s, cot_r)
    means.second()
    send(cot_s, cot_r, move_sems.at[0], move_sems.at[1], 2, 4)
    means.third()
    send(cot_s, cot_r, move_sems.at[0], move_sems.at[1], 4, 8)

    def project_values(i, carry):
        start = pl.multiple_of(i * 16, 16)
        flat = fields[pl.ds(start, 16)].reshape(16 * X, C)
        values[pl.ds(start, 16)] = dot(flat, w_value[...]).astype(BF).reshape(16, X, C)
        return carry

    lax.fori_loop(0, 4, project_values, 0)
    means.end()

    attention(pooled, w_query, w_key, 2, attn_x, kernel_x, back_x)

    def over_x(i, carry):
        start = pl.multiple_of(i * 16, 16)
        for t in range(0, 16, 8):
            lines = mix(kernel_x, [values[start + t + n] for n in range(8)])
            for n in range(8):
                held[t + n] = lines[n]
        after_s[:, pl.ds(start, 16), :] = jnp.swapaxes(held[...], 0, 1)
        return carry

    lax.fori_loop(0, 4, over_x, 0)
    send(after_s, after_r, move_sems.at[2], move_sems.at[3])
    keep(after_s, after_r)
    attention(pooled, w_query, w_key, 0, attn_z, kernel_z, back_z)
    attention(pooled, w_query, w_key, 1, attn_y, kernel_y, back_y)
    means.close()

    wait_all(cot_r, move_sems.at[1])

    def back_over_z(step, carry):
        side, start = lax.div(step, 2), pl.multiple_of(lax.rem(step, 2) * 16, 16)
        y_start = pl.multiple_of(step * 16, 16)
        lines = []
        for low in range(ZL):
            lines.append(
                jnp.stack(
                    [cot_r[g * GY + side, pl.ds(low * YL + start, 16), :] for g in range(GZ)], axis=0
                )
            )
        block = jnp.stack(lines, axis=1).reshape(Z, 16, C)
        turned = jnp.swapaxes(block, 0, 1)
        cot_y[pl.ds(y_start, 16)] = turned
        grad_mixed = dot_nt(turned.reshape(16 * Z, C), w_out[...]).astype(BF).reshape(16, Z, C)
        mixed_y[pl.ds(y_start, 16)] = grad_mixed
        for t in range(0, 16, 8):
            lines = mix(back_z, [grad_mixed[t + n] for n in range(8)])
            for n in range(8):
                held[t + n, pl.ds(0, Z), :] = lines[n]
        grad_y[:, pl.ds(y_start, 16), :] = jnp.swapaxes(held[:, pl.ds(0, Z), :], 0, 1)
        return carry

    lax.fori_loop(0, 8, back_over_z, 0)

    def back_over_y(step, carry):
        lines = mix(back_y, [grad_y[step * 8 + n] for n in range(8)])
        for n in range(8):
            for side in range(GY):
                grad_s[(step * 4 + n // 2) * GY + side, pl.ds(n % 2 * YL, YL), :] = lines[n][
                    side * YL : (side + 1) * YL
                ]
        return carry

    lax.fori_loop(0, Z // 8, back_over_y, 0)
    halves = (pl.ds(0, YL), pl.ds(YL, YL))
    for low in range(ZL):
        send(grad_s, grad_r, move_sems.at[4], move_sems.at[5 + low], part=halves[low])
    keep(grad_s, grad_r)

    score_z[...] = jnp.zeros_like(score_z)
    score_y[...] = jnp.zeros_like(score_y)
    sum1[pl.ds(2 * (Z + Y), C), :] = jnp.zeros((C, C), F32)
    wait_all(after_r, move_sems.at[3])

    def over_y(step, carry):
        lines = []
        for n in range(8):
            lines.append(
                jnp.concatenate(
                    [after_r[(step * 4 + n // 2) * GY + side, pl.ds(n % 2 * YL, YL), :] for side in range(GY)], axis=0
                )
            )
        done = mix(kernel_y, lines)
        for n in range(8):
            after_y[step * 8 + n] = done[n]
        score_y[...] += pair_up([grad_y[step * 8 + n] for n in range(8)], lines)
        return carry

    lax.fori_loop(0, Z // 8, over_y, 0)

    def over_z(step, carry):
        y_start = pl.multiple_of(step * 16, 16)
        lines = jnp.swapaxes(after_y[:, pl.ds(y_start, 16), :], 0, 1)
        grad_mixed = mixed_y[pl.ds(y_start, 16)]
        parts = []
        for t in range(0, 16, 8):
            group = [lines[t + n] for n in range(8)]
            parts += mix(kernel_z, group)
            score_z[...] += pair_up([grad_mixed[t + n] for n in range(8)], group)
        mixed = jnp.concatenate(parts, axis=0)
        sum1[pl.ds(2 * (Z + Y), C), :] += dot_tn(mixed, cot_y[pl.ds(y_start, 16)].reshape(16 * Z, C))
        return carry

    lax.fori_loop(0, 8, over_z, 0)
    pull(pooled, w_query, w_key, 0, attn_z, score_z, sum1, 0, Z)
    pull(pooled, w_query, w_key, 1, attn_y, score_y, sum1, 2 * Z, 2 * Z + Y)
    early = Sum(sum1, total1, near1, wide1, sums1)
    early.first()

    score_x[...] = jnp.zeros_like(score_x)
    sum2[pl.ds(2 * X, C), :] = jnp.zeros((C, C), F32)

    def home(i, carry):
        start = pl.multiple_of(i * 16, 16)
        grad_x = jnp.swapaxes(grad_r[:, pl.ds(start, 16), :], 0, 1)
        for t in range(0, 16, 8):
            group = [grad_x[t + n] for n in range(8)]
            lines = mix(back_x, group)
            for n in range(8):
                grad_values[start + t + n] = lines[n]
            score_x[...] += pair_up(group, [values[start + t + n] for n in range(8)])
        grad = grad_values[pl.ds(start, 16)].reshape(16 * X, C)
        sum2[pl.ds(2 * X, C), :] += dot_tn(fields[pl.ds(start, 16)].reshape(16 * X, C), grad)
        return carry

    wait_all(grad_r, move_sems.at[5], halves[0])
    lax.fori_loop(0, 2, home, 0)
    early.second()
    wait_all(grad_r, move_sems.at[6], halves[1])
    lax.fori_loop(2, 4, home, 0)
    pull(pooled, w_query, w_key, 2, attn_x, score_x, sum2, 0, X)
    late = Sum(sum2, total2, near2, wide2, sums2)
    late.first()
    store_values = pltpu.make_async_copy(grad_values, grad_values_out, store_sems.at[0])
    store_values.start()
    early.third()
    late.second()
    early.end()
    early_rest[pl.ds(0, C), :] = total1[pl.ds(2 * (Z + Y), C), :]
    early_rest[pl.ds(5 * C, X), :] = pooled[pl.ds(Z + Y, X), :]
    early_rest[pl.ds(6 * C, Z), :] = settle(pooled, w_query, w_key, 0, total1, 0, Z, early_rest, C, 3 * C)
    early_rest[pl.ds(6 * C + Z, Y), :] = settle(
        pooled, w_query, w_key, 1, total1, 2 * Z, 2 * Z + Y, early_rest, 2 * C, 4 * C
    )
    late.third()
    store_early = pltpu.make_async_copy(early_rest, rest_out.at[pl.ds(3 * C, 7 * C + Z)], store_sems.at[1])
    store_early.start()
    late.end()
    store_late = pltpu.make_async_copy(total2, rest_out.at[pl.ds(0, 3 * C)], store_sems.at[2])
    store_late.start()
    wait_all(cot_s, move_sems.at[0])
    wait_all(after_s, move_sems.at[2])
    wait_all(grad_s, move_sems.at[4])
    early.close()
    late.close()
    store_values.wait()
    store_early.wait()
    store_late.wait()


REST = 10 * C + Z


def finish_kernel(
    grad_values_in, rest_in, w_value_in, w_query_in, w_key_in,
    field_grad, value_grad, out_grad, query_grad, key_grad,
    grad_values, rest, w_value, w_query, w_key, query_x, key_x, done, load_sems, store_sems,
):
    gz, gy = lax.axis_index("gz"), lax.axis_index("gy")
    loads = [
        pltpu.make_async_copy(rest_in, rest, load_sems.at[4]),
        pltpu.make_async_copy(w_query_in.at[pl.ds(2, 1)], w_query, load_sems.at[5]),
        pltpu.make_async_copy(w_key_in.at[pl.ds(2, 1)], w_key, load_sems.at[6]),
        pltpu.make_async_copy(w_value_in, w_value, load_sems.at[7]),
    ]

    def part(src, dst, i, sem):
        return pltpu.make_async_copy(src.at[pl.ds(16 * i, 16)], dst.at[pl.ds(16 * i, 16)], sem)

    for copy in loads:
        copy.start()
    for i in range(4):
        part(grad_values_in, grad_values, i, load_sems.at[i]).start()
    for copy in loads:
        copy.wait()

    def block(i):
        return rest.at[pl.ds(C * i, C)]

    stores = [
        pltpu.make_async_copy(block(2), value_grad, store_sems.at[4]),
        pltpu.make_async_copy(block(3), out_grad, store_sems.at[5]),
        pltpu.make_async_copy(block(4), query_grad.at[0], store_sems.at[6]),
        pltpu.make_async_copy(block(5), query_grad.at[1], store_sems.at[7]),
        pltpu.make_async_copy(block(6), key_grad.at[0], store_sems.at[8]),
        pltpu.make_async_copy(block(7), key_grad.at[1], store_sems.at[9]),
        pltpu.make_async_copy(query_x, query_grad.at[2], store_sems.at[10]),
        pltpu.make_async_copy(key_x, key_grad.at[2], store_sems.at[11]),
    ]
    for copy in stores[:6]:
        copy.start()
    means = rest[pl.ds(8 * C, X), :] / COUNTS[2]
    scale = lax.rsqrt(jnp.mean(means * means, axis=-1, keepdims=True) + EPS)
    normed = means * scale
    grad_q, grad_k = rest[pl.ds(0, X), :], rest[pl.ds(X, X), :]
    query_x[...] = dot_tn(normed, grad_q, HIGH)
    key_x[...] = dot_tn(normed, grad_k, HIGH)
    for copy in stores[6:]:
        copy.start()
    grad = dot_nt(grad_q, w_query[0], HIGH) + dot_nt(grad_k, w_key[0], HIGH)
    inner = jnp.mean(grad * normed, axis=-1, keepdims=True)
    means_x = scale * (grad - normed * inner) / COUNTS[2]
    for i in range(4):
        part(grad_values_in, grad_values, i, load_sems.at[i]).wait()
        direct = dot_nt(grad_values[pl.ds(16 * i, 16)].reshape(16 * X, C), w_value[...]).reshape(16, X, C)
        part_z = rest[pl.ds(9 * C + gz * ZL + i // 2, 1), :]
        part_y = rest[pl.ds(pl.multiple_of(9 * C + Z + gy * YL + (i % 2) * 16, 16), 16), :]
        cells = part_z + part_y
        done[pl.ds(16 * i, 16)] = (direct + cells[:, None, :] + means_x[None]).astype(BF)
        part(done, field_grad, i, store_sems.at[i]).start()
    for i in range(4):
        part(done, field_grad, i, store_sems.at[i]).wait()
    for copy in stores:
        copy.wait()


def local(fields, cotangent, w_value, w_out, w_query, w_key):
    hbm = pl.BlockSpec(memory_space=pltpu.HBM)
    cells = (CELLS, X, C)
    blocks = (X, CELLS, C)
    sums = []
    for rows in (POOLED, 2 * (Z + Y) + C, 2 * X + C):
        sums += [
            pltpu.VMEM((rows, C), F32),
            pltpu.VMEM((rows, C), F32),
            pltpu.VMEM((8, rows // 8, C), F32),
            pltpu.VMEM((16, rows // 8, C), F32),
        ]
    map_shapes = []
    for length in LENGTHS:
        map_shapes += [
            pltpu.VMEM((H * length, length), F32),
            pltpu.VMEM((length, H * length), BF),
            pltpu.VMEM((length, H * length), BF),
        ]
    field_shapes = [
        cells, cells, blocks, blocks, (Y, Z, C), (Y, Z, C), (Z, Y, C), blocks, blocks, blocks, (Z, Y, C), blocks,
        cells, cells,
    ]
    weights = [pltpu.VMEM((C, C), BF)] * 2 + [pltpu.VMEM((3, C, C), F32)] * 2
    grad_values, rest = pl.pallas_call(
        whole_kernel,
        in_specs=[hbm] * 6,
        out_specs=[hbm] * 2,
        out_shape=[jax.ShapeDtypeStruct(cells, BF), jax.ShapeDtypeStruct((REST, C), F32)],
        scratch_shapes=[pltpu.VMEM(shape, BF) for shape in field_shapes]
        + [pltpu.VMEM((16, X, C), BF)]
        + weights
        + map_shapes
        + [
            pltpu.VMEM((H * Z, Z), F32),
            pltpu.VMEM((H * Y, Y), F32),
            pltpu.VMEM((H * X, X), F32),
            pltpu.VMEM((7 * C + Z, C), F32),
        ]
        + sums
        + [pltpu.SemaphoreType.DMA((count,)) for count in (12, 3, 7, 6, 6, 6)],
        compiler_params=params(collective_id=0, has_side_effects=True),
    )(fields.reshape(cells), cotangent.reshape(cells), w_value, w_out, w_query, w_key)
    square = jax.ShapeDtypeStruct((C, C), F32)
    cube = jax.ShapeDtypeStruct((3, C, C), F32)
    field_grad, value_grad, out_grad, query_grad, key_grad = pl.pallas_call(
        finish_kernel,
        in_specs=[hbm] * 5,
        out_specs=[hbm] * 5,
        out_shape=[jax.ShapeDtypeStruct(cells, BF), square, square, cube, cube],
        scratch_shapes=[
            pltpu.VMEM(cells, BF),
            pltpu.VMEM((REST, C), F32),
            pltpu.VMEM((C, C), BF),
            pltpu.VMEM((1, C, C), F32),
            pltpu.VMEM((1, C, C), F32),
            pltpu.VMEM((C, C), F32),
            pltpu.VMEM((C, C), F32),
            pltpu.VMEM(cells, BF),
            pltpu.SemaphoreType.DMA((8,)),
            pltpu.SemaphoreType.DMA((12,)),
        ],
        compiler_params=params(),
    )(grad_values, rest, w_value, w_query, w_key)
    return (field_grad.reshape(ZL, YL, X, C), value_grad, out_grad, query_grad, key_grad)


def solution(mesh):
    placed = (P("gz", "gy", None, None), P("gz", "gy", None, None), P(), P(), P(), P())
    return jax.shard_map(
        local,
        mesh=mesh,
        in_specs=placed,
        out_specs=(P("gz", "gy", None, None), P(), P(), P(), P()),
        check_vma=False,
    )
```

```python
import jax
import jax.numpy as jnp
from jax import lax
from jax.experimental import pallas as pl
from jax.experimental.pallas import tpu as pltpu
from jax.sharding import PartitionSpec as P

BF = jnp.bfloat16
F32 = jnp.float32
MESH = pl.DeviceIdType.MESH
H = 8
D = 16
C = 128
Z, Y, X = 64, 128, 128
ZL, YL = 2, 32
CELLS = ZL * YL
GZ, GY = 32, 4
EPS = 1e-06
HIGH = lax.Precision.HIGHEST
COUNTS = (Y * X, Z * X, Z * Y)
STARTS = (0, Z, Z + Y)
LENGTHS = (Z, Y, X)
POOLED = Z + Y + X
VMEM = pl.BlockSpec(memory_space=pltpu.VMEM)


def params(**more):
    return pltpu.CompilerParams(vmem_limit_bytes=56 * 2**20, **more)


def dot(a, b):
    return jnp.dot(a, b, preferred_element_type=F32)


def dot_nt(a, b, precision=None):
    return lax.dot_general(
        a, b, (((1,), (1,)), ((), ())), preferred_element_type=F32, precision=precision
    )


def dot_tn(a, b, precision=None):
    return lax.dot_general(
        a, b, (((0,), (0,)), ((), ())), preferred_element_type=F32, precision=precision
    )


def head_stack(block):
    head = lax.broadcasted_iota(jnp.int32, block.shape, 1) % C // D
    zero = jnp.zeros((), block.dtype)
    return jnp.concatenate([jnp.where(head == h, block, zero) for h in range(H)], axis=0)


def regroup(lines):
    group = lax.broadcasted_iota(jnp.int32, lines[0].shape, 1) // D
    for s in (1, 2, 4):
        low = group // s % 2 == 0
        found = list(lines)
        for k in range(8):
            if k // s % 2 == 0:
                a, b = lines[k], lines[k + s]
                found[k] = jnp.where(low, a, pltpu.roll(b, D * s, 1))
                found[k + s] = jnp.where(low, pltpu.roll(a, C - D * s, 1), b)
        lines = found
    return lines


def to_heads(lines):
    first, second = regroup(lines[:8]), regroup(lines[8:])
    return [jnp.concatenate([a, b], axis=1) for a, b in zip(first, second)]


def to_lines(heads):
    return regroup([head[:, :C] for head in heads]) + regroup([head[:, C:] for head in heads])


def mix(kernel, heads):
    length = heads[0].shape[0]
    done = [dot(kernel[h * length : (h + 1) * length], heads[h]).astype(BF) for h in range(H)]
    return to_lines(done)


def pair_up(score, left, right):
    length = left[0].shape[0]
    for h in range(H):
        score[pl.ds(h * length, length), :] += dot_nt(left[h], right[h])


def normalise(pooled, axis):
    means = pooled[pl.ds(STARTS[axis], LENGTHS[axis]), :] / COUNTS[axis]
    scale = lax.rsqrt(jnp.mean(means * means, axis=-1, keepdims=True) + EPS)
    return means * scale, scale


def project(normed, weight):
    return jnp.dot(normed, weight, preferred_element_type=F32, precision=HIGH)


def attention(pooled, w_query, w_key, axis, attn, kernel, back):
    length = LENGTHS[axis]
    normed, _ = normalise(pooled, axis)
    queries = project(normed, w_query[axis])
    keys = project(normed, w_key[axis])
    scores = dot_nt(head_stack(queries), keys, HIGH) * (1.0 / D**0.5)
    grown = jnp.exp(scores - jnp.max(scores, axis=-1, keepdims=True))
    soft = grown / jnp.sum(grown, axis=-1, keepdims=True)
    attn[...] = soft
    heads = [soft[h * length : (h + 1) * length] for h in range(H)]
    kernel[...] = soft.astype(BF)
    back[...] = jnp.concatenate([head.T for head in heads], axis=0).astype(BF)


def pull(pooled, w_query, w_key, axis, attn, score, out, row_q, row_k):
    length = LENGTHS[axis]
    normed, _ = normalise(pooled, axis)
    queries = head_stack(project(normed, w_query[axis]))
    keys = head_stack(project(normed, w_key[axis]))
    soft, grad = attn[...], score[...]
    inner = jnp.sum(soft * grad, axis=-1, keepdims=True)
    grad = soft * (grad - inner) * (1.0 / D**0.5)
    heads = [grad[h * length : (h + 1) * length] for h in range(H)]
    out[pl.ds(row_q, length), :] = jnp.dot(
        jnp.concatenate(heads, axis=1), keys, preferred_element_type=F32, precision=HIGH
    )
    out[pl.ds(row_k, length), :] = dot_tn(grad, queries, HIGH)


def settle(pooled, w_query, w_key, axis, total, row_q, row_k, out, out_q, out_k):
    length = LENGTHS[axis]
    normed, scale = normalise(pooled, axis)
    grad_q = total[pl.ds(row_q, length), :]
    grad_k = total[pl.ds(row_k, length), :]
    out[pl.ds(out_q, C), :] = dot_tn(normed, grad_q, HIGH)
    out[pl.ds(out_k, C), :] = dot_tn(normed, grad_k, HIGH)
    grad = dot_nt(grad_q, w_query[axis], HIGH) + dot_nt(grad_k, w_key[axis], HIGH)
    inner = jnp.mean(grad * normed, axis=-1, keepdims=True)
    return scale * (grad - normed * inner) / COUNTS[axis]


def torus():
    gz, gy = lax.axis_index("gz"), lax.axis_index("gy")
    z, y = lax.div(gz, 8), lax.rem(lax.div(gz, 2), 4)
    x, core = lax.div(gy, 2) * 2 + lax.rem(gz, 2), lax.rem(gy, 2)
    lines = [
        [(lax.rem(z + dz, 4) * 4 + lax.rem(y + dy, 4)) * 2 for dy in range(4)] for dz in range(4)
    ]
    return lines, x, core


def shifts(step, first=0):
    lines, x, core = torus()
    to_core = lax.rem(core + lax.rem(step, 2), 2)
    turn = x + lax.div(step, 2)
    sides = []
    for dx in range(4):
        to_x = lax.rem(turn + dx, 4)
        sides.append((lax.rem(to_x, 2), lax.div(to_x, 2) * 2 + to_core))
    found = []
    for j in range(first, 16):
        dz, dy = j % 4, (j // 4 + j) % 4
        low, gy = sides[(j // 4 + 2 * j) % 4]
        found.append((lines[dz][dy] + low, gy))
    return found


def each_device(visit, first, last):
    def step(i, carry):
        for device in shifts(i):
            visit(device)
        return carry

    if first == 0:
        for device in shifts(jnp.int32(0), 1):
            visit(device)
        first = 1
    lax.fori_loop(first, last, step, 0)


def mine():
    return lax.axis_index("gz") * GY + lax.axis_index("gy")


def wait_bytes(ref, sem):
    pltpu.make_async_copy(ref, ref, sem).wait()


def send(src, dst, send_sem, recv_sem, first=0, last=8, part=None):
    me = mine()

    def block(ref, index):
        return ref.at[index] if part is None else ref.at[index, part]

    def visit(device):
        pltpu.make_async_remote_copy(
            block(src, device[0] * GY + device[1]), block(dst, me), send_sem, recv_sem,
            device_id=device, device_id_type=MESH,
        ).start()

    each_device(visit, first, last)


def keep(src, dst):
    me = mine()
    dst[me] = src[me]


def wait_all(ref, sem, part=None):
    if part is None:
        wait_bytes(ref.at[pl.ds(0, 127)], sem)
    else:
        wait_bytes(ref.at[pl.ds(0, 127), part], sem)


class Sum:
    def __init__(self, src, out, near, wide, sems):
        self.src, self.out, self.near, self.wide, self.sems = src, out, near, wide, sems
        self.piece = src.shape[0] // 8
        gz, gy = lax.axis_index("gz"), lax.axis_index("gy")
        self.gz, self.gy = gz, gy
        self.line, self.side = lax.div(gz, 2), lax.rem(gz, 2) * 4 + gy

    def rows(self, index):
        return pl.ds(pl.multiple_of(index * self.piece, 8), self.piece)

    def near_peer(self, k):
        peer = lax.rem(self.side + k, 8)
        return peer, (self.line * 2 + lax.div(peer, 4), lax.rem(peer, 4))

    def wide_peer(self, k):
        peer = lax.rem(self.line + k, 16)
        return peer, (peer * 2 + lax.rem(self.gz, 2), self.gy)

    def copy(self, src, dst, first, device):
        pltpu.make_async_remote_copy(
            src, dst, self.sems.at[first], self.sems.at[first + 1], device_id=device, device_id_type=MESH
        ).start()

    def first(self):
        for k in range(1, 8):
            peer, device = self.near_peer(k)
            self.copy(self.src.at[self.rows(peer)], self.near.at[self.side], 0, device)
        self.near[self.side] = self.src[self.rows(self.side)]

    def second(self):
        wait_bytes(self.near.at[pl.ds(0, 7)], self.sems.at[1])
        self.wide[self.line] = jnp.sum(self.near[...], axis=0)
        for k in range(1, 16):
            peer, device = self.wide_peer(k)
            self.copy(self.wide.at[self.line], self.wide.at[self.line], 2, device)

    def third(self):
        wait_bytes(self.wide.at[pl.ds(0, 15)], self.sems.at[3])
        rows = self.rows(self.side)
        self.out[rows] = jnp.sum(self.wide[...], axis=0)
        for k in range(1, 8):
            peer, device = self.near_peer(k)
            self.copy(self.out.at[rows], self.out.at[rows], 4, device)

    def end(self):
        wait_bytes(self.near.at[pl.ds(0, 7)], self.sems.at[5])

    def close(self):
        wait_bytes(self.near.at[pl.ds(0, 7)], self.sems.at[0])
        wait_bytes(self.wide.at[pl.ds(0, 15)], self.sems.at[2])
        wait_bytes(self.near.at[pl.ds(0, 7)], self.sems.at[4])


def whole_kernel(
    fields_in, cot_in, w_value_in, w_out_in, w_query_in, w_key_in,
    grad_values_out, rest_out,
    fields, cot, cot_s, cot_r, cot_y, mixed_y, grad_y, grad_s, after_s, after_r, after_y, grad_r, values, grad_values,
    held, w_value, w_out, w_query, w_key,
    attn_z, kernel_z, back_z, attn_y, kernel_y, back_y, attn_x, kernel_x, back_x,
    score_z, score_y, score_x, early_rest,
    sum0, pooled, near0, wide0, sum1, total1, near1, wide1, sum2, total2, near2, wide2,
    load_sems, store_sems, move_sems, sums0, sums1, sums2, group_in,
):
    gz, gy = lax.axis_index("gz"), lax.axis_index("gy")

    def load(i, src, dst, base):
        return pltpu.make_async_copy(src.at[pl.ds(16 * i, 16)], dst.at[pl.ds(16 * i, 16)], load_sems.at[base + i])

    weights = [
        pltpu.make_async_copy(src, dst, load_sems.at[8 + i])
        for i, (src, dst) in enumerate(
            ((w_value_in, w_value), (w_out_in, w_out), (w_query_in, w_query), (w_key_in, w_key))
        )
    ]
    for i in range(4):
        load(i, fields_in, fields, 0).start()
    for i in range(4):
        load(i, cot_in, cot, 4).start()
    for copy in weights:
        copy.start()

    means = Sum(sum0, pooled, near0, wide0, sums0)
    barrier = pltpu.get_barrier_semaphore()
    for k in range(1, 8):
        pl.semaphore_signal(barrier, inc=1, device_id=means.near_peer(k)[1], device_id_type=MESH)
    for k in range(1, 16):
        pl.semaphore_signal(barrier, inc=1, device_id=means.wide_peer(k)[1], device_id_type=MESH)

    sum0[...] = jnp.zeros_like(sum0)
    for i in range(4):
        load(i, fields_in, fields, 0).wait()
        block = fields[pl.ds(16 * i, 16)].astype(F32)
        cells = jnp.sum(block, axis=1)
        sum0[pl.ds(Z + Y, X), :] += jnp.sum(block, axis=0)
        sum0[pl.ds(gz * ZL + i // 2, 1), :] += jnp.sum(cells, axis=0, keepdims=True)
        sum0[pl.ds(pl.multiple_of(Z + gy * YL + (i % 2) * 16, 16), 16), :] += cells
    pl.semaphore_wait(barrier, 22)
    means.first()
    for k in range(1, 16):
        pl.semaphore_signal(group_in, inc=1, device_id=means.wide_peer(k)[1], device_id_type=MESH)
    for i in range(4):
        load(i, cot_in, cot, 4).wait()
        cot_s[:, pl.ds(16 * i, 16), :] = jnp.swapaxes(cot[pl.ds(16 * i, 16)], 0, 1)
    pl.semaphore_wait(group_in, 15)
    send(cot_s, cot_r, move_sems.at[0], move_sems.at[1], 0, 2)
    keep(cot_s, cot_r)
    means.second()
    send(cot_s, cot_r, move_sems.at[0], move_sems.at[1], 2, 4)
    means.third()
    send(cot_s, cot_r, move_sems.at[0], move_sems.at[1], 4, 8)

    for copy in weights:
        copy.wait()

    def project_values(i, carry):
        start = pl.multiple_of(i * 16, 16)
        flat = fields[pl.ds(start, 16)].reshape(16 * X, C)
        values[pl.ds(start, 16)] = dot(flat, w_value[...]).astype(BF).reshape(16, X, C)
        return carry

    lax.fori_loop(0, 4, project_values, 0)
    means.end()

    attention(pooled, w_query, w_key, 2, attn_x, kernel_x, back_x)

    def over_x(i, carry):
        start = pl.multiple_of(i * 16, 16)
        lines = mix(kernel_x, to_heads([values[start + n] for n in range(16)]))
        for n in range(16):
            held[n] = lines[n]
        after_s[:, pl.ds(start, 16), :] = jnp.swapaxes(held[...], 0, 1)
        return carry

    lax.fori_loop(0, 4, over_x, 0)
    send(after_s, after_r, move_sems.at[2], move_sems.at[3])
    keep(after_s, after_r)
    attention(pooled, w_query, w_key, 0, attn_z, kernel_z, back_z)
    attention(pooled, w_query, w_key, 1, attn_y, kernel_y, back_y)
    means.close()

    wait_all(cot_r, move_sems.at[1])

    def back_over_z(step, carry):
        side, start = lax.div(step, 2), pl.multiple_of(lax.rem(step, 2) * 16, 16)
        y_start = pl.multiple_of(step * 16, 16)
        lines = []
        for low in range(ZL):
            lines.append(
                jnp.stack(
                    [cot_r[g * GY + side, pl.ds(low * YL + start, 16), :] for g in range(GZ)], axis=0
                )
            )
        block = jnp.stack(lines, axis=1).reshape(Z, 16, C)
        turned = jnp.swapaxes(block, 0, 1)
        cot_y[pl.ds(y_start, 16)] = turned
        grad_mixed = dot_nt(turned.reshape(16 * Z, C), w_out[...]).astype(BF).reshape(16, Z, C)
        mixed_y[pl.ds(y_start, 16)] = grad_mixed
        lines = mix(back_z, to_heads([grad_mixed[n] for n in range(16)]))
        for n in range(16):
            held[n, pl.ds(0, Z), :] = lines[n]
        grad_y[:, pl.ds(y_start, 16), :] = jnp.swapaxes(held[:, pl.ds(0, Z), :], 0, 1)
        return carry

    lax.fori_loop(0, 8, back_over_z, 0)

    def back_over_y(step, carry):
        lines = mix(back_y, to_heads([grad_y[step * 16 + n] for n in range(16)]))
        for n in range(16):
            for side in range(GY):
                grad_s[(step * 8 + n // 2) * GY + side, pl.ds(n % 2 * YL, YL), :] = lines[n][
                    side * YL : (side + 1) * YL
                ]
        return carry

    lax.fori_loop(0, Z // 16, back_over_y, 0)
    halves = (pl.ds(0, YL), pl.ds(YL, YL))
    for low in range(ZL):
        send(grad_s, grad_r, move_sems.at[4], move_sems.at[5 + low], part=halves[low])
    keep(grad_s, grad_r)

    score_z[...] = jnp.zeros_like(score_z)
    score_y[...] = jnp.zeros_like(score_y)
    sum1[pl.ds(2 * (Z + Y), C), :] = jnp.zeros((C, C), F32)
    wait_all(after_r, move_sems.at[3])

    def over_y(step, carry):
        lines = []
        for n in range(16):
            lines.append(
                jnp.concatenate(
                    [after_r[(step * 8 + n // 2) * GY + side, pl.ds(n % 2 * YL, YL), :] for side in range(GY)], axis=0
                )
            )
        heads = to_heads(lines)
        pair_up(score_y, to_heads([grad_y[step * 16 + n] for n in range(16)]), heads)
        done = mix(kernel_y, heads)
        for n in range(16):
            after_y[step * 16 + n] = done[n]
        return carry

    lax.fori_loop(0, Z // 16, over_y, 0)

    def over_z(step, carry):
        y_start = pl.multiple_of(step * 16, 16)
        lines = jnp.swapaxes(after_y[:, pl.ds(y_start, 16), :], 0, 1)
        grad_mixed = mixed_y[pl.ds(y_start, 16)]
        heads = to_heads([lines[n] for n in range(16)])
        pair_up(score_z, to_heads([grad_mixed[n] for n in range(16)]), heads)
        mixed = jnp.concatenate(mix(kernel_z, heads), axis=0)
        sum1[pl.ds(2 * (Z + Y), C), :] += dot_tn(mixed, cot_y[pl.ds(y_start, 16)].reshape(16 * Z, C))
        return carry

    lax.fori_loop(0, 8, over_z, 0)
    pull(pooled, w_query, w_key, 0, attn_z, score_z, sum1, 0, Z)
    pull(pooled, w_query, w_key, 1, attn_y, score_y, sum1, 2 * Z, 2 * Z + Y)
    early = Sum(sum1, total1, near1, wide1, sums1)
    early.first()

    score_x[...] = jnp.zeros_like(score_x)
    sum2[pl.ds(2 * X, C), :] = jnp.zeros((C, C), F32)

    def home(i, carry):
        start = pl.multiple_of(i * 16, 16)
        grad_x = jnp.swapaxes(grad_r[:, pl.ds(start, 16), :], 0, 1)
        heads = to_heads([grad_x[n] for n in range(16)])
        pair_up(score_x, heads, to_heads([values[start + n] for n in range(16)]))
        lines = mix(back_x, heads)
        for n in range(16):
            grad_values[start + n] = lines[n]
        grad = grad_values[pl.ds(start, 16)].reshape(16 * X, C)
        sum2[pl.ds(2 * X, C), :] += dot_tn(fields[pl.ds(start, 16)].reshape(16 * X, C), grad)
        return carry

    wait_all(grad_r, move_sems.at[5], halves[0])
    lax.fori_loop(0, 2, home, 0)
    wait_all(grad_r, move_sems.at[6], halves[1])
    early.second()
    lax.fori_loop(2, 4, home, 0)
    pull(pooled, w_query, w_key, 2, attn_x, score_x, sum2, 0, X)
    late = Sum(sum2, total2, near2, wide2, sums2)
    late.first()
    store_values = pltpu.make_async_copy(grad_values, grad_values_out, store_sems.at[0])
    store_values.start()
    early.third()
    late.second()
    early.end()
    early_rest[pl.ds(0, C), :] = total1[pl.ds(2 * (Z + Y), C), :]
    early_rest[pl.ds(5 * C, X), :] = pooled[pl.ds(Z + Y, X), :]
    early_rest[pl.ds(6 * C, Z), :] = settle(pooled, w_query, w_key, 0, total1, 0, Z, early_rest, C, 3 * C)
    early_rest[pl.ds(6 * C + Z, Y), :] = settle(
        pooled, w_query, w_key, 1, total1, 2 * Z, 2 * Z + Y, early_rest, 2 * C, 4 * C
    )
    late.third()
    store_early = pltpu.make_async_copy(early_rest, rest_out.at[pl.ds(3 * C, 7 * C + Z)], store_sems.at[1])
    store_early.start()
    late.end()
    store_late = pltpu.make_async_copy(total2, rest_out.at[pl.ds(0, 3 * C)], store_sems.at[2])
    store_late.start()
    wait_all(cot_s, move_sems.at[0])
    wait_all(after_s, move_sems.at[2])
    wait_all(grad_s, move_sems.at[4])
    early.close()
    late.close()
    store_values.wait()
    store_early.wait()
    store_late.wait()


REST = 10 * C + Z


def finish_kernel(
    grad_values_in, rest_in, w_value_in, w_query_in, w_key_in,
    field_grad, value_grad, out_grad, query_grad, key_grad,
    grad_values, rest, w_value, w_query, w_key, query_x, key_x, done, load_sems, store_sems,
):
    gz, gy = lax.axis_index("gz"), lax.axis_index("gy")
    loads = [
        pltpu.make_async_copy(rest_in, rest, load_sems.at[4]),
        pltpu.make_async_copy(w_query_in.at[pl.ds(2, 1)], w_query, load_sems.at[5]),
        pltpu.make_async_copy(w_key_in.at[pl.ds(2, 1)], w_key, load_sems.at[6]),
        pltpu.make_async_copy(w_value_in, w_value, load_sems.at[7]),
    ]

    def part(src, dst, i, sem):
        return pltpu.make_async_copy(src.at[pl.ds(16 * i, 16)], dst.at[pl.ds(16 * i, 16)], sem)

    for copy in loads:
        copy.start()
    for i in range(4):
        part(grad_values_in, grad_values, i, load_sems.at[i]).start()
    for copy in loads:
        copy.wait()

    def block(i):
        return rest.at[pl.ds(C * i, C)]

    stores = [
        pltpu.make_async_copy(block(2), value_grad, store_sems.at[4]),
        pltpu.make_async_copy(block(3), out_grad, store_sems.at[5]),
        pltpu.make_async_copy(block(4), query_grad.at[0], store_sems.at[6]),
        pltpu.make_async_copy(block(5), query_grad.at[1], store_sems.at[7]),
        pltpu.make_async_copy(block(6), key_grad.at[0], store_sems.at[8]),
        pltpu.make_async_copy(block(7), key_grad.at[1], store_sems.at[9]),
        pltpu.make_async_copy(query_x, query_grad.at[2], store_sems.at[10]),
        pltpu.make_async_copy(key_x, key_grad.at[2], store_sems.at[11]),
    ]
    for copy in stores[:6]:
        copy.start()
    means = rest[pl.ds(8 * C, X), :] / COUNTS[2]
    scale = lax.rsqrt(jnp.mean(means * means, axis=-1, keepdims=True) + EPS)
    normed = means * scale
    grad_q, grad_k = rest[pl.ds(0, X), :], rest[pl.ds(X, X), :]
    query_x[...] = dot_tn(normed, grad_q, HIGH)
    key_x[...] = dot_tn(normed, grad_k, HIGH)
    for copy in stores[6:]:
        copy.start()
    grad = dot_nt(grad_q, w_query[0], HIGH) + dot_nt(grad_k, w_key[0], HIGH)
    inner = jnp.mean(grad * normed, axis=-1, keepdims=True)
    means_x = scale * (grad - normed * inner) / COUNTS[2]
    for i in range(4):
        part(grad_values_in, grad_values, i, load_sems.at[i]).wait()
        direct = dot_nt(grad_values[pl.ds(16 * i, 16)].reshape(16 * X, C), w_value[...]).reshape(16, X, C)
        part_z = rest[pl.ds(9 * C + gz * ZL + i // 2, 1), :]
        part_y = rest[pl.ds(pl.multiple_of(9 * C + Z + gy * YL + (i % 2) * 16, 16), 16), :]
        cells = part_z + part_y
        done[pl.ds(16 * i, 16)] = (direct + cells[:, None, :] + means_x[None]).astype(BF)
        part(done, field_grad, i, store_sems.at[i]).start()
    for i in range(4):
        part(done, field_grad, i, store_sems.at[i]).wait()
    for copy in stores:
        copy.wait()


def local(fields, cotangent, w_value, w_out, w_query, w_key):
    hbm = pl.BlockSpec(memory_space=pltpu.HBM)
    cells = (CELLS, X, C)
    blocks = (X, CELLS, C)
    sums = []
    for rows in (POOLED, 2 * (Z + Y) + C, 2 * X + C):
        sums += [
            pltpu.VMEM((rows, C), F32),
            pltpu.VMEM((rows, C), F32),
            pltpu.VMEM((8, rows // 8, C), F32),
            pltpu.VMEM((16, rows // 8, C), F32),
        ]
    map_shapes = []
    for length in LENGTHS:
        map_shapes += [
            pltpu.VMEM((H * length, length), F32),
            pltpu.VMEM((H * length, length), BF),
            pltpu.VMEM((H * length, length), BF),
        ]
    field_shapes = [
        cells, cells, blocks, blocks, (Y, Z, C), (Y, Z, C), (Z, Y, C), blocks, blocks, blocks, (Z, Y, C), blocks,
        cells, cells,
    ]
    weights = [pltpu.VMEM((C, C), BF)] * 2 + [pltpu.VMEM((3, C, C), F32)] * 2
    grad_values, rest = pl.pallas_call(
        whole_kernel,
        in_specs=[hbm] * 6,
        out_specs=[hbm] * 2,
        out_shape=[jax.ShapeDtypeStruct(cells, BF), jax.ShapeDtypeStruct((REST, C), F32)],
        scratch_shapes=[pltpu.VMEM(shape, BF) for shape in field_shapes]
        + [pltpu.VMEM((16, X, C), BF)]
        + weights
        + map_shapes
        + [
            pltpu.VMEM((H * Z, Z), F32),
            pltpu.VMEM((H * Y, Y), F32),
            pltpu.VMEM((H * X, X), F32),
            pltpu.VMEM((7 * C + Z, C), F32),
        ]
        + sums
        + [pltpu.SemaphoreType.DMA((count,)) for count in (12, 3, 7, 6, 6, 6)]
        + [pltpu.SemaphoreType.REGULAR],
        compiler_params=params(collective_id=0, has_side_effects=True),
    )(fields.reshape(cells), cotangent.reshape(cells), w_value, w_out, w_query, w_key)
    square = jax.ShapeDtypeStruct((C, C), F32)
    cube = jax.ShapeDtypeStruct((3, C, C), F32)
    field_grad, value_grad, out_grad, query_grad, key_grad = pl.pallas_call(
        finish_kernel,
        in_specs=[hbm] * 5,
        out_specs=[hbm] * 5,
        out_shape=[jax.ShapeDtypeStruct(cells, BF), square, square, cube, cube],
        scratch_shapes=[
            pltpu.VMEM(cells, BF),
            pltpu.VMEM((REST, C), F32),
            pltpu.VMEM((C, C), BF),
            pltpu.VMEM((1, C, C), F32),
            pltpu.VMEM((1, C, C), F32),
            pltpu.VMEM((C, C), F32),
            pltpu.VMEM((C, C), F32),
            pltpu.VMEM(cells, BF),
            pltpu.SemaphoreType.DMA((8,)),
            pltpu.SemaphoreType.DMA((12,)),
        ],
        compiler_params=params(),
    )(grad_values, rest, w_value, w_query, w_key)
    return (field_grad.reshape(ZL, YL, X, C), value_grad, out_grad, query_grad, key_grad)


def solution(mesh):
    placed = (P("gz", "gy", None, None), P("gz", "gy", None, None), P(), P(), P(), P())
    return jax.shard_map(
        local,
        mesh=mesh,
        in_specs=placed,
        out_specs=(P("gz", "gy", None, None), P(), P(), P(), P()),
        check_vma=False,
    )
```

```python
import jax
import jax.numpy as jnp
from jax import lax
from jax.experimental import pallas as pl
from jax.experimental.pallas import tpu as pltpu
from jax.sharding import PartitionSpec as P

BF = jnp.bfloat16
F32 = jnp.float32
MESH = pl.DeviceIdType.MESH
H = 8
D = 16
C = 128
Z, Y, X = 64, 128, 128
ZL, YL = 2, 32
CELLS = ZL * YL
GZ, GY = 32, 4
EPS = 1e-06
HIGH = lax.Precision.HIGHEST
COUNTS = (Y * X, Z * X, Z * Y)
STARTS = (0, Z, Z + Y)
LENGTHS = (Z, Y, X)
POOLED = Z + Y + X
VMEM = pl.BlockSpec(memory_space=pltpu.VMEM)


def params(**more):
    return pltpu.CompilerParams(vmem_limit_bytes=56 * 2**20, **more)


def dot(a, b):
    return jnp.dot(a, b, preferred_element_type=F32)


def dot_nt(a, b, precision=None):
    return lax.dot_general(
        a, b, (((1,), (1,)), ((), ())), preferred_element_type=F32, precision=precision
    )


def dot_tn(a, b, precision=None):
    return lax.dot_general(
        a, b, (((0,), (0,)), ((), ())), preferred_element_type=F32, precision=precision
    )


def head_stack(block):
    head = lax.broadcasted_iota(jnp.int32, block.shape, 1) % C // D
    zero = jnp.zeros((), block.dtype)
    return jnp.concatenate([jnp.where(head == h, block, zero) for h in range(H)], axis=0)


def head_of(shape):
    return lax.broadcasted_iota(jnp.int32, shape, 1) % C // D


def sides(length):
    return 4 if length == Z else 2


def arrange(heads):
    g = sides(heads[0].shape[0])
    return jnp.concatenate([jnp.concatenate(heads[p : p + g], axis=1) for p in range(0, H, g)], axis=0)


def mix(kernel, lines):
    length = lines[0].shape[0]
    g = sides(length)
    block = jnp.concatenate(lines, axis=1)
    head = head_of(block.shape)
    zero = jnp.zeros((), BF)
    deep = jnp.concatenate([jnp.where(head % g == r, block, zero) for r in range(g)], axis=0)
    tall = dot(kernel[...], deep)
    done = tall[:length]
    for p in range(1, H // g):
        done = jnp.where(head // g == p, tall[p * length : (p + 1) * length], done)
    done = done.astype(BF)
    return [done[:, C * t : C * (t + 1)] for t in range(len(lines))]


def pair_up(left, right):
    g = sides(left[0].shape[0])
    left, right = jnp.concatenate(left, axis=1), jnp.concatenate(right, axis=1)
    head = head_of(left.shape)
    zero = jnp.zeros((), BF)
    tall = jnp.concatenate([jnp.where(head // g == p, left, zero) for p in range(H // g)], axis=0)
    wide = jnp.concatenate([jnp.where(head % g == r, right, zero) for r in range(g)], axis=0)
    return dot_nt(tall, wide)


def apart(score, length):
    g = sides(length)
    heads = []
    for h in range(H):
        p, r = h // g, h % g
        heads.append(score[p * length : (p + 1) * length, r * length : (r + 1) * length])
    return jnp.concatenate(heads, axis=0)


def normalise(pooled, axis):
    means = pooled[pl.ds(STARTS[axis], LENGTHS[axis]), :] / COUNTS[axis]
    scale = lax.rsqrt(jnp.mean(means * means, axis=-1, keepdims=True) + EPS)
    return means * scale, scale


def project(normed, weight):
    return jnp.dot(normed, weight, preferred_element_type=F32, precision=HIGH)


def attention(pooled, w_query, w_key, axis, attn, kernel, back):
    length = LENGTHS[axis]
    normed, _ = normalise(pooled, axis)
    queries = project(normed, w_query[axis])
    keys = project(normed, w_key[axis])
    scores = dot_nt(head_stack(queries), keys, HIGH) * (1.0 / D**0.5)
    grown = jnp.exp(scores - jnp.max(scores, axis=-1, keepdims=True))
    soft = grown / jnp.sum(grown, axis=-1, keepdims=True)
    attn[...] = soft
    heads = [soft[h * length : (h + 1) * length] for h in range(H)]
    kernel[...] = arrange(heads).astype(BF)
    back[...] = arrange([head.T for head in heads]).astype(BF)


def pull(pooled, w_query, w_key, axis, attn, score, out, row_q, row_k):
    length = LENGTHS[axis]
    normed, _ = normalise(pooled, axis)
    queries = head_stack(project(normed, w_query[axis]))
    keys = head_stack(project(normed, w_key[axis]))
    soft, grad = attn[...], apart(score[...], length)
    inner = jnp.sum(soft * grad, axis=-1, keepdims=True)
    grad = soft * (grad - inner) * (1.0 / D**0.5)
    heads = [grad[h * length : (h + 1) * length] for h in range(H)]
    out[pl.ds(row_q, length), :] = jnp.dot(
        jnp.concatenate(heads, axis=1), keys, preferred_element_type=F32, precision=HIGH
    )
    out[pl.ds(row_k, length), :] = dot_tn(grad, queries, HIGH)


def settle(pooled, w_query, w_key, axis, total, row_q, row_k, out, out_q, out_k):
    length = LENGTHS[axis]
    normed, scale = normalise(pooled, axis)
    grad_q = total[pl.ds(row_q, length), :]
    grad_k = total[pl.ds(row_k, length), :]
    out[pl.ds(out_q, C), :] = dot_tn(normed, grad_q, HIGH)
    out[pl.ds(out_k, C), :] = dot_tn(normed, grad_k, HIGH)
    grad = dot_nt(grad_q, w_query[axis], HIGH) + dot_nt(grad_k, w_key[axis], HIGH)
    inner = jnp.mean(grad * normed, axis=-1, keepdims=True)
    return scale * (grad - normed * inner) / COUNTS[axis]


def torus():
    gz, gy = lax.axis_index("gz"), lax.axis_index("gy")
    z, y = lax.div(gz, 8), lax.rem(lax.div(gz, 2), 4)
    x, core = lax.div(gy, 2) * 2 + lax.rem(gz, 2), lax.rem(gy, 2)
    lines = [
        [(lax.rem(z + dz, 4) * 4 + lax.rem(y + dy, 4)) * 2 for dy in range(4)] for dz in range(4)
    ]
    return lines, x, core


def shifts(step, first=0):
    lines, x, core = torus()
    to_core = lax.rem(core + lax.rem(step, 2), 2)
    turn = x + lax.div(step, 2)
    sides = []
    for dx in range(4):
        to_x = lax.rem(turn + dx, 4)
        sides.append((lax.rem(to_x, 2), lax.div(to_x, 2) * 2 + to_core))
    found = []
    for j in range(first, 16):
        dz, dy = j % 4, (j // 4 + j) % 4
        low, gy = sides[(j // 4 + 2 * j) % 4]
        found.append((lines[dz][dy] + low, gy))
    return found


def each_device(visit, first, last):
    def step(i, carry):
        for device in shifts(i):
            visit(device)
        return carry

    if first == 0:
        for device in shifts(jnp.int32(0), 1):
            visit(device)
        first = 1
    lax.fori_loop(first, last, step, 0)


def mine():
    return lax.axis_index("gz") * GY + lax.axis_index("gy")


def wait_bytes(ref, sem):
    pltpu.make_async_copy(ref, ref, sem).wait()


def send(src, dst, send_sem, recv_sem, first=0, last=8, part=None):
    me = mine()

    def block(ref, index):
        return ref.at[index] if part is None else ref.at[index, part]

    def visit(device):
        pltpu.make_async_remote_copy(
            block(src, device[0] * GY + device[1]), block(dst, me), send_sem, recv_sem,
            device_id=device, device_id_type=MESH,
        ).start()

    each_device(visit, first, last)


def keep(src, dst):
    me = mine()
    dst[me] = src[me]


def wait_all(ref, sem, part=None):
    if part is None:
        wait_bytes(ref.at[pl.ds(0, 127)], sem)
    else:
        wait_bytes(ref.at[pl.ds(0, 127), part], sem)


class Sum:
    def __init__(self, src, out, near, wide, sems):
        self.src, self.out, self.near, self.wide, self.sems = src, out, near, wide, sems
        self.piece = src.shape[0] // 8
        gz, gy = lax.axis_index("gz"), lax.axis_index("gy")
        self.gz, self.gy = gz, gy
        self.line, self.side = lax.div(gz, 2), lax.rem(gz, 2) * 4 + gy

    def rows(self, index):
        return pl.ds(pl.multiple_of(index * self.piece, 8), self.piece)

    def near_peer(self, k):
        peer = lax.rem(self.side + k, 8)
        return peer, (self.line * 2 + lax.div(peer, 4), lax.rem(peer, 4))

    def wide_peer(self, k):
        peer = lax.rem(self.line + k, 16)
        return peer, (peer * 2 + lax.rem(self.gz, 2), self.gy)

    def copy(self, src, dst, first, device):
        pltpu.make_async_remote_copy(
            src, dst, self.sems.at[first], self.sems.at[first + 1], device_id=device, device_id_type=MESH
        ).start()

    def first(self):
        for k in range(1, 8):
            peer, device = self.near_peer(k)
            self.copy(self.src.at[self.rows(peer)], self.near.at[self.side], 0, device)
        self.near[self.side] = self.src[self.rows(self.side)]

    def second(self):
        wait_bytes(self.near.at[pl.ds(0, 7)], self.sems.at[1])
        self.wide[self.line] = jnp.sum(self.near[...], axis=0)
        for k in range(1, 16):
            peer, device = self.wide_peer(k)
            self.copy(self.wide.at[self.line], self.wide.at[self.line], 2, device)

    def third(self):
        wait_bytes(self.wide.at[pl.ds(0, 15)], self.sems.at[3])
        rows = self.rows(self.side)
        self.out[rows] = jnp.sum(self.wide[...], axis=0)
        for k in range(1, 8):
            peer, device = self.near_peer(k)
            self.copy(self.out.at[rows], self.out.at[rows], 4, device)

    def end(self):
        wait_bytes(self.near.at[pl.ds(0, 7)], self.sems.at[5])

    def close(self):
        wait_bytes(self.near.at[pl.ds(0, 7)], self.sems.at[0])
        wait_bytes(self.wide.at[pl.ds(0, 15)], self.sems.at[2])
        wait_bytes(self.near.at[pl.ds(0, 7)], self.sems.at[4])


def whole_kernel(
    fields_in, cot_in, w_value_in, w_out_in, w_query_in, w_key_in,
    grad_values_out, rest_out,
    fields, cot, cot_s, cot_r, cot_y, mixed_y, grad_y, grad_s, after_s, after_r, after_y, grad_r, values, grad_values,
    held, w_value, w_out, w_query, w_key,
    attn_z, kernel_z, back_z, attn_y, kernel_y, back_y, attn_x, kernel_x, back_x,
    score_z, score_y, score_x, early_rest,
    sum0, pooled, near0, wide0, sum1, total1, near1, wide1, sum2, total2, near2, wide2,
    load_sems, store_sems, move_sems, sums0, sums1, sums2, group_in,
):
    gz, gy = lax.axis_index("gz"), lax.axis_index("gy")

    def load(i, src, dst, base):
        return pltpu.make_async_copy(src.at[pl.ds(16 * i, 16)], dst.at[pl.ds(16 * i, 16)], load_sems.at[base + i])

    weights = [
        pltpu.make_async_copy(src, dst, load_sems.at[8 + i])
        for i, (src, dst) in enumerate(
            ((w_value_in, w_value), (w_out_in, w_out), (w_query_in, w_query), (w_key_in, w_key))
        )
    ]
    for i in range(4):
        load(i, fields_in, fields, 0).start()
    for i in range(4):
        load(i, cot_in, cot, 4).start()
    for copy in weights:
        copy.start()

    means = Sum(sum0, pooled, near0, wide0, sums0)
    barrier = pltpu.get_barrier_semaphore()
    for k in range(1, 8):
        pl.semaphore_signal(barrier, inc=1, device_id=means.near_peer(k)[1], device_id_type=MESH)
    for k in range(1, 16):
        pl.semaphore_signal(barrier, inc=1, device_id=means.wide_peer(k)[1], device_id_type=MESH)

    sum0[...] = jnp.zeros_like(sum0)
    for i in range(4):
        load(i, fields_in, fields, 0).wait()
        block = fields[pl.ds(16 * i, 16)].astype(F32)
        cells = jnp.sum(block, axis=1)
        sum0[pl.ds(Z + Y, X), :] += jnp.sum(block, axis=0)
        sum0[pl.ds(gz * ZL + i // 2, 1), :] += jnp.sum(cells, axis=0, keepdims=True)
        sum0[pl.ds(pl.multiple_of(Z + gy * YL + (i % 2) * 16, 16), 16), :] += cells
    for copy in weights:
        copy.wait()

    def project_values(i, carry):
        start = pl.multiple_of(i * 16, 16)
        flat = fields[pl.ds(start, 16)].reshape(16 * X, C)
        values[pl.ds(start, 16)] = dot(flat, w_value[...]).astype(BF).reshape(16, X, C)
        return carry

    lax.fori_loop(0, 4, project_values, 0)
    pl.semaphore_wait(barrier, 22)
    means.first()
    for k in range(1, 16):
        pl.semaphore_signal(group_in, inc=1, device_id=means.wide_peer(k)[1], device_id_type=MESH)
    for i in range(4):
        load(i, cot_in, cot, 4).wait()
        cot_s[:, pl.ds(16 * i, 16), :] = jnp.swapaxes(cot[pl.ds(16 * i, 16)], 0, 1)
    pl.semaphore_wait(group_in, 15)
    send(cot_s, cot_r, move_sems.at[0], move_sems.at[1], 0, 1)
    keep(cot_s, cot_r)
    means.second()
    send(cot_s, cot_r, move_sems.at[0], move_sems.at[1], 1, 3)
    means.third()
    send(cot_s, cot_r, move_sems.at[0], move_sems.at[1], 3, 8)

    means.end()

    attention(pooled, w_query, w_key, 2, attn_x, kernel_x, back_x)

    def over_x(i, carry):
        start = pl.multiple_of(i * 16, 16)
        for t in range(0, 16, 8):
            lines = mix(kernel_x, [values[start + t + n] for n in range(8)])
            for n in range(8):
                held[t + n] = lines[n]
        after_s[:, pl.ds(start, 16), :] = jnp.swapaxes(held[...], 0, 1)
        return carry

    lax.fori_loop(0, 4, over_x, 0)
    send(after_s, after_r, move_sems.at[2], move_sems.at[3])
    keep(after_s, after_r)
    attention(pooled, w_query, w_key, 0, attn_z, kernel_z, back_z)
    attention(pooled, w_query, w_key, 1, attn_y, kernel_y, back_y)
    means.close()

    wait_all(cot_r, move_sems.at[1])

    def back_over_z(step, carry):
        side, start = lax.div(step, 2), pl.multiple_of(lax.rem(step, 2) * 16, 16)
        y_start = pl.multiple_of(step * 16, 16)
        lines = []
        for low in range(ZL):
            lines.append(
                jnp.stack(
                    [cot_r[g * GY + side, pl.ds(low * YL + start, 16), :] for g in range(GZ)], axis=0
                )
            )
        block = jnp.stack(lines, axis=1).reshape(Z, 16, C)
        turned = jnp.swapaxes(block, 0, 1)
        cot_y[pl.ds(y_start, 16)] = turned
        grad_mixed = dot_nt(turned.reshape(16 * Z, C), w_out[...]).astype(BF).reshape(16, Z, C)
        mixed_y[pl.ds(y_start, 16)] = grad_mixed
        for t in range(0, 16, 8):
            lines = mix(back_z, [grad_mixed[t + n] for n in range(8)])
            for n in range(8):
                held[t + n, pl.ds(0, Z), :] = lines[n]
        grad_y[:, pl.ds(y_start, 16), :] = jnp.swapaxes(held[:, pl.ds(0, Z), :], 0, 1)
        return carry

    lax.fori_loop(0, 8, back_over_z, 0)

    def back_over_y(step, carry):
        lines = mix(back_y, [grad_y[step * 8 + n] for n in range(8)])
        for n in range(8):
            for side in range(GY):
                grad_s[(step * 4 + n // 2) * GY + side, pl.ds(n % 2 * YL, YL), :] = lines[n][
                    side * YL : (side + 1) * YL
                ]
        return carry

    lax.fori_loop(0, Z // 8, back_over_y, 0)
    halves = (pl.ds(0, YL), pl.ds(YL, YL))
    for low in range(ZL):
        send(grad_s, grad_r, move_sems.at[4], move_sems.at[5 + low], part=halves[low])
    keep(grad_s, grad_r)

    score_z[...] = jnp.zeros_like(score_z)
    score_y[...] = jnp.zeros_like(score_y)
    sum1[pl.ds(2 * (Z + Y), C), :] = jnp.zeros((C, C), F32)
    wait_all(after_r, move_sems.at[3])

    def over_y(step, carry):
        lines = []
        for n in range(8):
            lines.append(
                jnp.concatenate(
                    [after_r[(step * 4 + n // 2) * GY + side, pl.ds(n % 2 * YL, YL), :] for side in range(GY)], axis=0
                )
            )
        done = mix(kernel_y, lines)
        for n in range(8):
            after_y[step * 8 + n] = done[n]
        score_y[...] += pair_up([grad_y[step * 8 + n] for n in range(8)], lines)
        return carry

    lax.fori_loop(0, Z // 8, over_y, 0)

    def over_z(step, carry):
        y_start = pl.multiple_of(step * 16, 16)
        lines = jnp.swapaxes(after_y[:, pl.ds(y_start, 16), :], 0, 1)
        grad_mixed = mixed_y[pl.ds(y_start, 16)]
        parts = []
        for t in range(0, 16, 8):
            group = [lines[t + n] for n in range(8)]
            parts += mix(kernel_z, group)
            score_z[...] += pair_up([grad_mixed[t + n] for n in range(8)], group)
        mixed = jnp.concatenate(parts, axis=0)
        sum1[pl.ds(2 * (Z + Y), C), :] += dot_tn(mixed, cot_y[pl.ds(y_start, 16)].reshape(16 * Z, C))
        return carry

    lax.fori_loop(0, 8, over_z, 0)
    pull(pooled, w_query, w_key, 0, attn_z, score_z, sum1, 0, Z)
    pull(pooled, w_query, w_key, 1, attn_y, score_y, sum1, 2 * Z, 2 * Z + Y)
    early = Sum(sum1, total1, near1, wide1, sums1)
    early.first()

    score_x[...] = jnp.zeros_like(score_x)
    sum2[pl.ds(2 * X, C), :] = jnp.zeros((C, C), F32)

    def home(i, carry):
        start = pl.multiple_of(i * 16, 16)
        grad_x = jnp.swapaxes(grad_r[:, pl.ds(start, 16), :], 0, 1)
        for t in range(0, 16, 8):
            group = [grad_x[t + n] for n in range(8)]
            lines = mix(back_x, group)
            for n in range(8):
                grad_values[start + t + n] = lines[n]
            score_x[...] += pair_up(group, [values[start + t + n] for n in range(8)])
        grad = grad_values[pl.ds(start, 16)].reshape(16 * X, C)
        sum2[pl.ds(2 * X, C), :] += dot_tn(fields[pl.ds(start, 16)].reshape(16 * X, C), grad)
        return carry

    wait_all(grad_r, move_sems.at[5], halves[0])
    lax.fori_loop(0, 2, home, 0)
    wait_all(grad_r, move_sems.at[6], halves[1])
    early.second()
    lax.fori_loop(2, 4, home, 0)
    pull(pooled, w_query, w_key, 2, attn_x, score_x, sum2, 0, X)
    late = Sum(sum2, total2, near2, wide2, sums2)
    late.first()
    store_values = pltpu.make_async_copy(grad_values, grad_values_out, store_sems.at[0])
    store_values.start()
    early.third()
    late.second()
    early.end()
    early_rest[pl.ds(0, C), :] = total1[pl.ds(2 * (Z + Y), C), :]
    early_rest[pl.ds(5 * C, X), :] = pooled[pl.ds(Z + Y, X), :]
    early_rest[pl.ds(6 * C, Z), :] = settle(pooled, w_query, w_key, 0, total1, 0, Z, early_rest, C, 3 * C)
    early_rest[pl.ds(6 * C + Z, Y), :] = settle(
        pooled, w_query, w_key, 1, total1, 2 * Z, 2 * Z + Y, early_rest, 2 * C, 4 * C
    )
    late.third()
    store_early = pltpu.make_async_copy(early_rest, rest_out.at[pl.ds(3 * C, 7 * C + Z)], store_sems.at[1])
    store_early.start()
    late.end()
    store_late = pltpu.make_async_copy(total2, rest_out.at[pl.ds(0, 3 * C)], store_sems.at[2])
    store_late.start()
    wait_all(cot_s, move_sems.at[0])
    wait_all(after_s, move_sems.at[2])
    wait_all(grad_s, move_sems.at[4])
    early.close()
    late.close()
    store_values.wait()
    store_early.wait()
    store_late.wait()


REST = 10 * C + Z


def finish_kernel(
    grad_values_in, rest_in, w_value_in, w_query_in, w_key_in,
    field_grad, value_grad, out_grad, query_grad, key_grad,
    grad_values, rest, w_value, w_query, w_key, query_x, key_x, done, load_sems, store_sems,
):
    gz, gy = lax.axis_index("gz"), lax.axis_index("gy")
    loads = [
        pltpu.make_async_copy(rest_in, rest, load_sems.at[4]),
        pltpu.make_async_copy(w_query_in.at[pl.ds(2, 1)], w_query, load_sems.at[5]),
        pltpu.make_async_copy(w_key_in.at[pl.ds(2, 1)], w_key, load_sems.at[6]),
        pltpu.make_async_copy(w_value_in, w_value, load_sems.at[7]),
    ]

    def part(src, dst, i, sem):
        return pltpu.make_async_copy(src.at[pl.ds(16 * i, 16)], dst.at[pl.ds(16 * i, 16)], sem)

    for copy in loads:
        copy.start()
    for i in range(4):
        part(grad_values_in, grad_values, i, load_sems.at[i]).start()
    for copy in loads:
        copy.wait()

    def block(i):
        return rest.at[pl.ds(C * i, C)]

    stores = [
        pltpu.make_async_copy(block(2), value_grad, store_sems.at[4]),
        pltpu.make_async_copy(block(3), out_grad, store_sems.at[5]),
        pltpu.make_async_copy(block(4), query_grad.at[0], store_sems.at[6]),
        pltpu.make_async_copy(block(5), query_grad.at[1], store_sems.at[7]),
        pltpu.make_async_copy(block(6), key_grad.at[0], store_sems.at[8]),
        pltpu.make_async_copy(block(7), key_grad.at[1], store_sems.at[9]),
        pltpu.make_async_copy(query_x, query_grad.at[2], store_sems.at[10]),
        pltpu.make_async_copy(key_x, key_grad.at[2], store_sems.at[11]),
    ]
    for copy in stores[:6]:
        copy.start()
    means = rest[pl.ds(8 * C, X), :] / COUNTS[2]
    scale = lax.rsqrt(jnp.mean(means * means, axis=-1, keepdims=True) + EPS)
    normed = means * scale
    grad_q, grad_k = rest[pl.ds(0, X), :], rest[pl.ds(X, X), :]
    query_x[...] = dot_tn(normed, grad_q, HIGH)
    key_x[...] = dot_tn(normed, grad_k, HIGH)
    for copy in stores[6:]:
        copy.start()
    grad = dot_nt(grad_q, w_query[0], HIGH) + dot_nt(grad_k, w_key[0], HIGH)
    inner = jnp.mean(grad * normed, axis=-1, keepdims=True)
    means_x = scale * (grad - normed * inner) / COUNTS[2]
    for i in range(4):
        part(grad_values_in, grad_values, i, load_sems.at[i]).wait()
        direct = dot_nt(grad_values[pl.ds(16 * i, 16)].reshape(16 * X, C), w_value[...]).reshape(16, X, C)
        part_z = rest[pl.ds(9 * C + gz * ZL + i // 2, 1), :]
        part_y = rest[pl.ds(pl.multiple_of(9 * C + Z + gy * YL + (i % 2) * 16, 16), 16), :]
        cells = part_z + part_y
        done[pl.ds(16 * i, 16)] = (direct + cells[:, None, :] + means_x[None]).astype(BF)
        part(done, field_grad, i, store_sems.at[i]).start()
    for i in range(4):
        part(done, field_grad, i, store_sems.at[i]).wait()
    for copy in stores:
        copy.wait()


def local(fields, cotangent, w_value, w_out, w_query, w_key):
    hbm = pl.BlockSpec(memory_space=pltpu.HBM)
    cells = (CELLS, X, C)
    blocks = (X, CELLS, C)
    sums = []
    for rows in (POOLED, 2 * (Z + Y) + C, 2 * X + C):
        sums += [
            pltpu.VMEM((rows, C), F32),
            pltpu.VMEM((rows, C), F32),
            pltpu.VMEM((8, rows // 8, C), F32),
            pltpu.VMEM((16, rows // 8, C), F32),
        ]
    map_shapes = []
    for length in LENGTHS:
        map_shapes += [
            pltpu.VMEM((H * length, length), F32),
            pltpu.VMEM((H // sides(length) * length, sides(length) * length), BF),
            pltpu.VMEM((H // sides(length) * length, sides(length) * length), BF),
        ]
    field_shapes = [
        cells, cells, blocks, blocks, (Y, Z, C), (Y, Z, C), (Z, Y, C), blocks, blocks, blocks, (Z, Y, C), blocks,
        cells, cells,
    ]
    weights = [pltpu.VMEM((C, C), BF)] * 2 + [pltpu.VMEM((3, C, C), F32)] * 2
    grad_values, rest = pl.pallas_call(
        whole_kernel,
        in_specs=[hbm] * 6,
        out_specs=[hbm] * 2,
        out_shape=[jax.ShapeDtypeStruct(cells, BF), jax.ShapeDtypeStruct((REST, C), F32)],
        scratch_shapes=[pltpu.VMEM(shape, BF) for shape in field_shapes]
        + [pltpu.VMEM((16, X, C), BF)]
        + weights
        + map_shapes
        + [
            pltpu.VMEM((H // sides(Z) * Z, sides(Z) * Z), F32),
            pltpu.VMEM((H // sides(Y) * Y, sides(Y) * Y), F32),
            pltpu.VMEM((H // sides(X) * X, sides(X) * X), F32),
            pltpu.VMEM((7 * C + Z, C), F32),
        ]
        + sums
        + [pltpu.SemaphoreType.DMA((count,)) for count in (12, 3, 7, 6, 6, 6)]
        + [pltpu.SemaphoreType.REGULAR],
        compiler_params=params(collective_id=0, has_side_effects=True),
    )(fields.reshape(cells), cotangent.reshape(cells), w_value, w_out, w_query, w_key)
    square = jax.ShapeDtypeStruct((C, C), F32)
    cube = jax.ShapeDtypeStruct((3, C, C), F32)
    field_grad, value_grad, out_grad, query_grad, key_grad = pl.pallas_call(
        finish_kernel,
        in_specs=[hbm] * 5,
        out_specs=[hbm] * 5,
        out_shape=[jax.ShapeDtypeStruct(cells, BF), square, square, cube, cube],
        scratch_shapes=[
            pltpu.VMEM(cells, BF),
            pltpu.VMEM((REST, C), F32),
            pltpu.VMEM((C, C), BF),
            pltpu.VMEM((1, C, C), F32),
            pltpu.VMEM((1, C, C), F32),
            pltpu.VMEM((C, C), F32),
            pltpu.VMEM((C, C), F32),
            pltpu.VMEM(cells, BF),
            pltpu.SemaphoreType.DMA((8,)),
            pltpu.SemaphoreType.DMA((12,)),
        ],
        compiler_params=params(),
    )(grad_values, rest, w_value, w_query, w_key)
    return (field_grad.reshape(ZL, YL, X, C), value_grad, out_grad, query_grad, key_grad)


def solution(mesh):
    placed = (P("gz", "gy", None, None), P("gz", "gy", None, None), P(), P(), P(), P())
    return jax.shard_map(
        local,
        mesh=mesh,
        in_specs=placed,
        out_specs=(P("gz", "gy", None, None), P(), P(), P(), P()),
        check_vma=False,
    )
```

```python
import jax
import jax.numpy as jnp
from jax import lax
from jax.experimental import pallas as pl
from jax.experimental.pallas import tpu as pltpu
from jax.sharding import PartitionSpec as P

BF = jnp.bfloat16
F32 = jnp.float32
MESH = pl.DeviceIdType.MESH
H = 8
D = 16
C = 128
Z, Y, X = 64, 128, 128
ZL, YL = 2, 32
CELLS = ZL * YL
GZ, GY = 32, 4
EPS = 1e-06
NEAR = (8, 16, 16)
HIGH = lax.Precision.HIGHEST
COUNTS = (Y * X, Z * X, Z * Y)
STARTS = (0, Z, Z + Y)
LENGTHS = (Z, Y, X)
POOLED = Z + Y + X
VMEM = pl.BlockSpec(memory_space=pltpu.VMEM)


def params(**more):
    return pltpu.CompilerParams(vmem_limit_bytes=56 * 2**20, **more)


def dot(a, b):
    return jnp.dot(a, b, preferred_element_type=F32)


def dot_nt(a, b, precision=None):
    return lax.dot_general(
        a, b, (((1,), (1,)), ((), ())), preferred_element_type=F32, precision=precision
    )


def dot_tn(a, b, precision=None):
    return lax.dot_general(
        a, b, (((0,), (0,)), ((), ())), preferred_element_type=F32, precision=precision
    )


def head_stack(block):
    head = lax.broadcasted_iota(jnp.int32, block.shape, 1) % C // D
    zero = jnp.zeros((), block.dtype)
    return jnp.concatenate([jnp.where(head == h, block, zero) for h in range(H)], axis=0)


def head_of(shape):
    return lax.broadcasted_iota(jnp.int32, shape, 1) % C // D


def sides(length):
    return 4 if length == Z else 2


def arrange(heads):
    g = sides(heads[0].shape[0])
    return jnp.concatenate([jnp.concatenate(heads[p : p + g], axis=1) for p in range(0, H, g)], axis=0)


def mix(kernel, lines):
    length = lines[0].shape[0]
    g = sides(length)
    block = jnp.concatenate(lines, axis=1)
    head = head_of(block.shape)
    zero = jnp.zeros((), BF)
    deep = jnp.concatenate([jnp.where(head % g == r, block, zero) for r in range(g)], axis=0)
    tall = dot(kernel[...], deep)
    done = tall[:length]
    for p in range(1, H // g):
        done = jnp.where(head // g == p, tall[p * length : (p + 1) * length], done)
    done = done.astype(BF)
    return [done[:, C * t : C * (t + 1)] for t in range(len(lines))]


def pair_up(left, right):
    g = sides(left[0].shape[0])
    left, right = jnp.concatenate(left, axis=1), jnp.concatenate(right, axis=1)
    head = head_of(left.shape)
    zero = jnp.zeros((), BF)
    tall = jnp.concatenate([jnp.where(head // g == p, left, zero) for p in range(H // g)], axis=0)
    wide = jnp.concatenate([jnp.where(head % g == r, right, zero) for r in range(g)], axis=0)
    return dot_nt(tall, wide)


def apart(score, length):
    g = sides(length)
    heads = []
    for h in range(H):
        p, r = h // g, h % g
        heads.append(score[p * length : (p + 1) * length, r * length : (r + 1) * length])
    return jnp.concatenate(heads, axis=0)


def normalise(pooled, axis):
    means = pooled[pl.ds(STARTS[axis], LENGTHS[axis]), :] / COUNTS[axis]
    scale = lax.rsqrt(jnp.mean(means * means, axis=-1, keepdims=True) + EPS)
    return means * scale, scale


def project(normed, weight):
    return jnp.dot(normed, weight, preferred_element_type=F32, precision=HIGH)


def attention(pooled, w_query, w_key, axis, attn, kernel, back):
    length = LENGTHS[axis]
    normed, _ = normalise(pooled, axis)
    queries = project(normed, w_query[axis])
    keys = project(normed, w_key[axis])
    scores = dot_nt(head_stack(queries), keys, HIGH) * (1.0 / D**0.5)
    grown = jnp.exp(scores - jnp.max(scores, axis=-1, keepdims=True))
    soft = grown / jnp.sum(grown, axis=-1, keepdims=True)
    attn[...] = soft
    heads = [soft[h * length : (h + 1) * length] for h in range(H)]
    kernel[...] = arrange(heads).astype(BF)
    back[...] = arrange([head.T for head in heads]).astype(BF)


def pull(pooled, w_query, w_key, axis, attn, score, out, row_q, row_k):
    length = LENGTHS[axis]
    normed, _ = normalise(pooled, axis)
    queries = head_stack(project(normed, w_query[axis]))
    keys = head_stack(project(normed, w_key[axis]))
    soft, grad = attn[...], apart(score[...], length)
    inner = jnp.sum(soft * grad, axis=-1, keepdims=True)
    grad = soft * (grad - inner) * (1.0 / D**0.5)
    heads = [grad[h * length : (h + 1) * length] for h in range(H)]
    out[pl.ds(row_q, length), :] = jnp.dot(
        jnp.concatenate(heads, axis=1), keys, preferred_element_type=F32, precision=HIGH
    )
    out[pl.ds(row_k, length), :] = dot_tn(grad, queries, HIGH)


def settle(pooled, w_query, w_key, axis, total, row_q, row_k, out, out_q, out_k):
    length = LENGTHS[axis]
    normed, scale = normalise(pooled, axis)
    grad_q = total[pl.ds(row_q, length), :]
    grad_k = total[pl.ds(row_k, length), :]
    out[pl.ds(out_q, C), :] = dot_tn(normed, grad_q, HIGH)
    out[pl.ds(out_k, C), :] = dot_tn(normed, grad_k, HIGH)
    grad = dot_nt(grad_q, w_query[axis], HIGH) + dot_nt(grad_k, w_key[axis], HIGH)
    inner = jnp.mean(grad * normed, axis=-1, keepdims=True)
    return scale * (grad - normed * inner) / COUNTS[axis]


def torus():
    gz, gy = lax.axis_index("gz"), lax.axis_index("gy")
    z, y = lax.div(gz, 8), lax.rem(lax.div(gz, 2), 4)
    x, core = lax.div(gy, 2) * 2 + lax.rem(gz, 2), lax.rem(gy, 2)
    lines = [
        [(lax.rem(z + dz, 4) * 4 + lax.rem(y + dy, 4)) * 2 for dy in range(4)] for dz in range(4)
    ]
    return lines, x, core


def shifts(step, first=0):
    lines, x, core = torus()
    to_core = lax.rem(core + lax.rem(step, 2), 2)
    turn = x + lax.div(step, 2)
    sides = []
    for dx in range(4):
        to_x = lax.rem(turn + dx, 4)
        sides.append((lax.rem(to_x, 2), lax.div(to_x, 2) * 2 + to_core))
    found = []
    for j in range(first, 16):
        dz, dy = j % 4, (j // 4 + j) % 4
        low, gy = sides[(j // 4 + 2 * j) % 4]
        found.append((lines[dz][dy] + low, gy))
    return found


def each_device(visit, first, last):
    def step(i, carry):
        for device in shifts(i):
            visit(device)
        return carry

    if first == 0:
        for device in shifts(jnp.int32(0), 1):
            visit(device)
        first = 1
    lax.fori_loop(first, last, step, 0)


def mine():
    return lax.axis_index("gz") * GY + lax.axis_index("gy")


def wait_bytes(ref, sem):
    pltpu.make_async_copy(ref, ref, sem).wait()


def send(src, dst, send_sem, recv_sem, first=0, last=8, part=None):
    me = mine()

    def block(ref, index):
        return ref.at[index] if part is None else ref.at[index, part]

    def visit(device):
        pltpu.make_async_remote_copy(
            block(src, device[0] * GY + device[1]), block(dst, me), send_sem, recv_sem,
            device_id=device, device_id_type=MESH,
        ).start()

    each_device(visit, first, last)


def keep(src, dst):
    me = mine()
    dst[me] = src[me]


def wait_all(ref, sem, part=None):
    if part is None:
        wait_bytes(ref.at[pl.ds(0, 127)], sem)
    else:
        wait_bytes(ref.at[pl.ds(0, 127), part], sem)


class Sum:
    def __init__(self, src, out, near, wide, sems):
        self.src, self.out, self.near, self.wide, self.sems = src, out, near, wide, sems
        self.near_size, self.wide_size = near.shape[0], wide.shape[0]
        self.piece = src.shape[0] // self.near_size
        self.lows = self.near_size // 4
        gz, gy = lax.axis_index("gz"), lax.axis_index("gy")
        self.low, self.gy = lax.rem(gz, self.lows), gy
        self.line, self.side = lax.div(gz, self.lows), self.low * 4 + gy

    def rows(self, index):
        return pl.ds(pl.multiple_of(index * self.piece, 8), self.piece)

    def near_peer(self, k):
        peer = lax.rem(self.side + k, self.near_size)
        return peer, (self.line * self.lows + lax.div(peer, 4), lax.rem(peer, 4))

    def wide_peer(self, k):
        peer = lax.rem(self.line + k, self.wide_size)
        return peer, (peer * self.lows + self.low, self.gy)

    def copy(self, src, dst, first, device):
        pltpu.make_async_remote_copy(
            src, dst, self.sems.at[first], self.sems.at[first + 1], device_id=device, device_id_type=MESH
        ).start()

    def first(self):
        for k in range(1, self.near_size):
            peer, device = self.near_peer(k)
            self.copy(self.src.at[self.rows(peer)], self.near.at[self.side], 0, device)
        self.near[self.side] = self.src[self.rows(self.side)]

    def second(self):
        wait_bytes(self.near.at[pl.ds(0, self.near_size - 1)], self.sems.at[1])
        self.wide[self.line] = jnp.sum(self.near[...], axis=0)
        for k in range(1, self.wide_size):
            peer, device = self.wide_peer(k)
            self.copy(self.wide.at[self.line], self.wide.at[self.line], 2, device)

    def third(self):
        wait_bytes(self.wide.at[pl.ds(0, self.wide_size - 1)], self.sems.at[3])
        rows = self.rows(self.side)
        self.out[rows] = jnp.sum(self.wide[...], axis=0)
        for k in range(1, self.near_size):
            peer, device = self.near_peer(k)
            self.copy(self.out.at[rows], self.out.at[rows], 4, device)

    def end(self):
        wait_bytes(self.near.at[pl.ds(0, self.near_size - 1)], self.sems.at[5])

    def close(self):
        wait_bytes(self.near.at[pl.ds(0, self.near_size - 1)], self.sems.at[0])
        wait_bytes(self.wide.at[pl.ds(0, self.wide_size - 1)], self.sems.at[2])
        wait_bytes(self.near.at[pl.ds(0, self.near_size - 1)], self.sems.at[4])


def whole_kernel(
    fields_in, cot_in, w_value_in, w_out_in, w_query_in, w_key_in,
    grad_values_out, rest_out,
    fields, cot, cot_s, cot_r, cot_y, mixed_y, grad_y, grad_s, after_s, after_r, after_y, grad_r, values, grad_values,
    held, w_value, w_out, w_query, w_key,
    attn_z, kernel_z, back_z, attn_y, kernel_y, back_y, attn_x, kernel_x, back_x,
    score_z, score_y, score_x, early_rest,
    sum0, pooled, near0, wide0, sum1, total1, near1, wide1, sum2, total2, near2, wide2,
    load_sems, store_sems, move_sems, sums0, sums1, sums2, group_in,
):
    gz, gy = lax.axis_index("gz"), lax.axis_index("gy")

    def load(i, src, dst, base):
        return pltpu.make_async_copy(src.at[pl.ds(16 * i, 16)], dst.at[pl.ds(16 * i, 16)], load_sems.at[base + i])

    weights = [
        pltpu.make_async_copy(src, dst, load_sems.at[8 + i])
        for i, (src, dst) in enumerate(
            ((w_value_in, w_value), (w_out_in, w_out), (w_query_in, w_query), (w_key_in, w_key))
        )
    ]
    for i in range(4):
        load(i, fields_in, fields, 0).start()
    for i in range(4):
        load(i, cot_in, cot, 4).start()
    for copy in weights:
        copy.start()

    means = Sum(sum0, pooled, near0, wide0, sums0)
    barrier = pltpu.get_barrier_semaphore()
    for k in range(1, 8):
        pl.semaphore_signal(barrier, inc=1, device_id=means.near_peer(k)[1], device_id_type=MESH)
    for k in range(1, 16):
        pl.semaphore_signal(barrier, inc=1, device_id=means.wide_peer(k)[1], device_id_type=MESH)
    other = lax.div(gz, 4) * 4 + 2 - lax.div(lax.rem(gz, 4), 2) * 2
    for k in range(1, 8):
        device = (other + lax.rem(lax.rem(gz, 2) + k // 4, 2), lax.rem(gy + k % 4, 4))
        pl.semaphore_signal(barrier, inc=1, device_id=device, device_id_type=MESH)

    sum0[...] = jnp.zeros_like(sum0)
    for i in range(4):
        load(i, fields_in, fields, 0).wait()
        block = fields[pl.ds(16 * i, 16)].astype(F32)
        cells = jnp.sum(block, axis=1)
        sum0[pl.ds(Z + Y, X), :] += jnp.sum(block, axis=0)
        sum0[pl.ds(gz * ZL + i // 2, 1), :] += jnp.sum(cells, axis=0, keepdims=True)
        sum0[pl.ds(pl.multiple_of(Z + gy * YL + (i % 2) * 16, 16), 16), :] += cells
    for copy in weights:
        copy.wait()

    def project_values(i, carry):
        start = pl.multiple_of(i * 16, 16)
        flat = fields[pl.ds(start, 16)].reshape(16 * X, C)
        values[pl.ds(start, 16)] = dot(flat, w_value[...]).astype(BF).reshape(16, X, C)
        return carry

    lax.fori_loop(0, 4, project_values, 0)
    pl.semaphore_wait(barrier, 29)
    means.first()
    for k in range(1, 16):
        pl.semaphore_signal(group_in, inc=1, device_id=means.wide_peer(k)[1], device_id_type=MESH)
    for i in range(4):
        load(i, cot_in, cot, 4).wait()
        cot_s[:, pl.ds(16 * i, 16), :] = jnp.swapaxes(cot[pl.ds(16 * i, 16)], 0, 1)
    pl.semaphore_wait(group_in, 15)
    send(cot_s, cot_r, move_sems.at[0], move_sems.at[1], 0, 1)
    keep(cot_s, cot_r)
    means.second()
    send(cot_s, cot_r, move_sems.at[0], move_sems.at[1], 1, 3)
    means.third()
    send(cot_s, cot_r, move_sems.at[0], move_sems.at[1], 3, 8)

    means.end()

    attention(pooled, w_query, w_key, 2, attn_x, kernel_x, back_x)

    def over_x(i, carry):
        start = pl.multiple_of(i * 16, 16)
        for t in range(0, 16, 8):
            lines = mix(kernel_x, [values[start + t + n] for n in range(8)])
            for n in range(8):
                held[t + n] = lines[n]
        after_s[:, pl.ds(start, 16), :] = jnp.swapaxes(held[...], 0, 1)
        return carry

    lax.fori_loop(0, 4, over_x, 0)
    send(after_s, after_r, move_sems.at[2], move_sems.at[3])
    keep(after_s, after_r)
    attention(pooled, w_query, w_key, 0, attn_z, kernel_z, back_z)
    attention(pooled, w_query, w_key, 1, attn_y, kernel_y, back_y)
    means.close()

    wait_all(cot_r, move_sems.at[1])

    def back_over_z(step, carry):
        side, start = lax.div(step, 2), pl.multiple_of(lax.rem(step, 2) * 16, 16)
        y_start = pl.multiple_of(step * 16, 16)
        lines = []
        for low in range(ZL):
            lines.append(
                jnp.stack(
                    [cot_r[g * GY + side, pl.ds(low * YL + start, 16), :] for g in range(GZ)], axis=0
                )
            )
        block = jnp.stack(lines, axis=1).reshape(Z, 16, C)
        turned = jnp.swapaxes(block, 0, 1)
        cot_y[pl.ds(y_start, 16)] = turned
        grad_mixed = dot_nt(turned.reshape(16 * Z, C), w_out[...]).astype(BF).reshape(16, Z, C)
        mixed_y[pl.ds(y_start, 16)] = grad_mixed
        for t in range(0, 16, 8):
            lines = mix(back_z, [grad_mixed[t + n] for n in range(8)])
            for n in range(8):
                held[t + n, pl.ds(0, Z), :] = lines[n]
        grad_y[:, pl.ds(y_start, 16), :] = jnp.swapaxes(held[:, pl.ds(0, Z), :], 0, 1)
        return carry

    lax.fori_loop(0, 8, back_over_z, 0)

    def back_over_y(step, carry):
        lines = mix(back_y, [grad_y[step * 8 + n] for n in range(8)])
        for n in range(8):
            for side in range(GY):
                grad_s[(step * 4 + n // 2) * GY + side, pl.ds(n % 2 * YL, YL), :] = lines[n][
                    side * YL : (side + 1) * YL
                ]
        return carry

    lax.fori_loop(0, Z // 8, back_over_y, 0)
    halves = (pl.ds(0, YL), pl.ds(YL, YL))
    for low in range(ZL):
        send(grad_s, grad_r, move_sems.at[4], move_sems.at[5 + low], part=halves[low])
    keep(grad_s, grad_r)

    score_z[...] = jnp.zeros_like(score_z)
    score_y[...] = jnp.zeros_like(score_y)
    sum1[pl.ds(2 * (Z + Y), C), :] = jnp.zeros((C, C), F32)
    wait_all(after_r, move_sems.at[3])

    def over_y(step, carry):
        lines = []
        for n in range(8):
            lines.append(
                jnp.concatenate(
                    [after_r[(step * 4 + n // 2) * GY + side, pl.ds(n % 2 * YL, YL), :] for side in range(GY)], axis=0
                )
            )
        done = mix(kernel_y, lines)
        for n in range(8):
            after_y[step * 8 + n] = done[n]
        score_y[...] += pair_up([grad_y[step * 8 + n] for n in range(8)], lines)
        return carry

    lax.fori_loop(0, Z // 8, over_y, 0)

    def over_z(step, carry):
        y_start = pl.multiple_of(step * 16, 16)
        lines = jnp.swapaxes(after_y[:, pl.ds(y_start, 16), :], 0, 1)
        grad_mixed = mixed_y[pl.ds(y_start, 16)]
        parts = []
        for t in range(0, 16, 8):
            group = [lines[t + n] for n in range(8)]
            parts += mix(kernel_z, group)
            score_z[...] += pair_up([grad_mixed[t + n] for n in range(8)], group)
        mixed = jnp.concatenate(parts, axis=0)
        sum1[pl.ds(2 * (Z + Y), C), :] += dot_tn(mixed, cot_y[pl.ds(y_start, 16)].reshape(16 * Z, C))
        return carry

    lax.fori_loop(0, 8, over_z, 0)
    pull(pooled, w_query, w_key, 0, attn_z, score_z, sum1, 0, Z)
    pull(pooled, w_query, w_key, 1, attn_y, score_y, sum1, 2 * Z, 2 * Z + Y)
    early = Sum(sum1, total1, near1, wide1, sums1)
    early.first()

    score_x[...] = jnp.zeros_like(score_x)
    sum2[pl.ds(2 * X, C), :] = jnp.zeros((C, C), F32)

    def home(i, carry):
        start = pl.multiple_of(i * 16, 16)
        grad_x = jnp.swapaxes(grad_r[:, pl.ds(start, 16), :], 0, 1)
        for t in range(0, 16, 8):
            group = [grad_x[t + n] for n in range(8)]
            lines = mix(back_x, group)
            for n in range(8):
                grad_values[start + t + n] = lines[n]
            score_x[...] += pair_up(group, [values[start + t + n] for n in range(8)])
        grad = grad_values[pl.ds(start, 16)].reshape(16 * X, C)
        sum2[pl.ds(2 * X, C), :] += dot_tn(fields[pl.ds(start, 16)].reshape(16 * X, C), grad)
        return carry

    wait_all(grad_r, move_sems.at[5], halves[0])
    lax.fori_loop(0, 2, home, 0)
    wait_all(grad_r, move_sems.at[6], halves[1])
    lax.fori_loop(2, 4, home, 0)
    early.second()
    pull(pooled, w_query, w_key, 2, attn_x, score_x, sum2, 0, X)
    late = Sum(sum2, total2, near2, wide2, sums2)
    late.first()
    store_values = pltpu.make_async_copy(grad_values, grad_values_out, store_sems.at[0])
    store_values.start()
    late.second()
    early.third()
    late.third()
    early.end()
    early_rest[pl.ds(0, C), :] = total1[pl.ds(2 * (Z + Y), C), :]
    early_rest[pl.ds(5 * C, X), :] = pooled[pl.ds(Z + Y, X), :]
    early_rest[pl.ds(6 * C, Z), :] = settle(pooled, w_query, w_key, 0, total1, 0, Z, early_rest, C, 3 * C)
    early_rest[pl.ds(6 * C + Z, Y), :] = settle(
        pooled, w_query, w_key, 1, total1, 2 * Z, 2 * Z + Y, early_rest, 2 * C, 4 * C
    )
    store_early = pltpu.make_async_copy(early_rest, rest_out.at[pl.ds(3 * C, 7 * C + Z)], store_sems.at[1])
    store_early.start()
    late.end()
    store_late = pltpu.make_async_copy(total2, rest_out.at[pl.ds(0, 3 * C)], store_sems.at[2])
    store_late.start()
    wait_all(cot_s, move_sems.at[0])
    wait_all(after_s, move_sems.at[2])
    wait_all(grad_s, move_sems.at[4])
    early.close()
    late.close()
    store_values.wait()
    store_early.wait()
    store_late.wait()


REST = 10 * C + Z


def finish_kernel(
    grad_values_in, rest_in, w_value_in, w_query_in, w_key_in,
    field_grad, value_grad, out_grad, query_grad, key_grad,
    grad_values, rest, w_value, w_query, w_key, query_x, key_x, done, load_sems, store_sems,
):
    gz, gy = lax.axis_index("gz"), lax.axis_index("gy")
    loads = [
        pltpu.make_async_copy(rest_in, rest, load_sems.at[4]),
        pltpu.make_async_copy(w_query_in.at[pl.ds(2, 1)], w_query, load_sems.at[5]),
        pltpu.make_async_copy(w_key_in.at[pl.ds(2, 1)], w_key, load_sems.at[6]),
        pltpu.make_async_copy(w_value_in, w_value, load_sems.at[7]),
    ]

    def part(src, dst, i, sem):
        return pltpu.make_async_copy(src.at[pl.ds(16 * i, 16)], dst.at[pl.ds(16 * i, 16)], sem)

    for copy in loads:
        copy.start()
    for i in range(4):
        part(grad_values_in, grad_values, i, load_sems.at[i]).start()
    for copy in loads:
        copy.wait()

    def block(i):
        return rest.at[pl.ds(C * i, C)]

    stores = [
        pltpu.make_async_copy(block(2), value_grad, store_sems.at[4]),
        pltpu.make_async_copy(block(3), out_grad, store_sems.at[5]),
        pltpu.make_async_copy(block(4), query_grad.at[0], store_sems.at[6]),
        pltpu.make_async_copy(block(5), query_grad.at[1], store_sems.at[7]),
        pltpu.make_async_copy(block(6), key_grad.at[0], store_sems.at[8]),
        pltpu.make_async_copy(block(7), key_grad.at[1], store_sems.at[9]),
        pltpu.make_async_copy(query_x, query_grad.at[2], store_sems.at[10]),
        pltpu.make_async_copy(key_x, key_grad.at[2], store_sems.at[11]),
    ]
    for copy in stores[:6]:
        copy.start()
    means = rest[pl.ds(8 * C, X), :] / COUNTS[2]
    scale = lax.rsqrt(jnp.mean(means * means, axis=-1, keepdims=True) + EPS)
    normed = means * scale
    grad_q, grad_k = rest[pl.ds(0, X), :], rest[pl.ds(X, X), :]
    query_x[...] = dot_tn(normed, grad_q, HIGH)
    key_x[...] = dot_tn(normed, grad_k, HIGH)
    for copy in stores[6:]:
        copy.start()
    grad = dot_nt(grad_q, w_query[0], HIGH) + dot_nt(grad_k, w_key[0], HIGH)
    inner = jnp.mean(grad * normed, axis=-1, keepdims=True)
    means_x = scale * (grad - normed * inner) / COUNTS[2]
    for i in range(4):
        part(grad_values_in, grad_values, i, load_sems.at[i]).wait()
        direct = dot_nt(grad_values[pl.ds(16 * i, 16)].reshape(16 * X, C), w_value[...]).reshape(16, X, C)
        part_z = rest[pl.ds(9 * C + gz * ZL + i // 2, 1), :]
        part_y = rest[pl.ds(pl.multiple_of(9 * C + Z + gy * YL + (i % 2) * 16, 16), 16), :]
        cells = part_z + part_y
        done[pl.ds(16 * i, 16)] = (direct + cells[:, None, :] + means_x[None]).astype(BF)
        part(done, field_grad, i, store_sems.at[i]).start()
    for i in range(4):
        part(done, field_grad, i, store_sems.at[i]).wait()
    for copy in stores:
        copy.wait()


def local(fields, cotangent, w_value, w_out, w_query, w_key):
    hbm = pl.BlockSpec(memory_space=pltpu.HBM)
    cells = (CELLS, X, C)
    blocks = (X, CELLS, C)
    sums = []
    for rows, near in zip((POOLED, 2 * (Z + Y) + C, 2 * X + C), NEAR):
        sums += [
            pltpu.VMEM((rows, C), F32),
            pltpu.VMEM((rows, C), F32),
            pltpu.VMEM((near, rows // near, C), F32),
            pltpu.VMEM((128 // near, rows // near, C), F32),
        ]
    map_shapes = []
    for length in LENGTHS:
        map_shapes += [
            pltpu.VMEM((H * length, length), F32),
            pltpu.VMEM((H // sides(length) * length, sides(length) * length), BF),
            pltpu.VMEM((H // sides(length) * length, sides(length) * length), BF),
        ]
    field_shapes = [
        cells, cells, blocks, blocks, (Y, Z, C), (Y, Z, C), (Z, Y, C), blocks, blocks, blocks, (Z, Y, C), blocks,
        cells, cells,
    ]
    weights = [pltpu.VMEM((C, C), BF)] * 2 + [pltpu.VMEM((3, C, C), F32)] * 2
    grad_values, rest = pl.pallas_call(
        whole_kernel,
        in_specs=[hbm] * 6,
        out_specs=[hbm] * 2,
        out_shape=[jax.ShapeDtypeStruct(cells, BF), jax.ShapeDtypeStruct((REST, C), F32)],
        scratch_shapes=[pltpu.VMEM(shape, BF) for shape in field_shapes]
        + [pltpu.VMEM((16, X, C), BF)]
        + weights
        + map_shapes
        + [
            pltpu.VMEM((H // sides(Z) * Z, sides(Z) * Z), F32),
            pltpu.VMEM((H // sides(Y) * Y, sides(Y) * Y), F32),
            pltpu.VMEM((H // sides(X) * X, sides(X) * X), F32),
            pltpu.VMEM((7 * C + Z, C), F32),
        ]
        + sums
        + [pltpu.SemaphoreType.DMA((count,)) for count in (12, 3, 7, 6, 6, 6)]
        + [pltpu.SemaphoreType.REGULAR],
        compiler_params=params(collective_id=0, has_side_effects=True),
    )(fields.reshape(cells), cotangent.reshape(cells), w_value, w_out, w_query, w_key)
    square = jax.ShapeDtypeStruct((C, C), F32)
    cube = jax.ShapeDtypeStruct((3, C, C), F32)
    field_grad, value_grad, out_grad, query_grad, key_grad = pl.pallas_call(
        finish_kernel,
        in_specs=[hbm] * 5,
        out_specs=[hbm] * 5,
        out_shape=[jax.ShapeDtypeStruct(cells, BF), square, square, cube, cube],
        scratch_shapes=[
            pltpu.VMEM(cells, BF),
            pltpu.VMEM((REST, C), F32),
            pltpu.VMEM((C, C), BF),
            pltpu.VMEM((1, C, C), F32),
            pltpu.VMEM((1, C, C), F32),
            pltpu.VMEM((C, C), F32),
            pltpu.VMEM((C, C), F32),
            pltpu.VMEM(cells, BF),
            pltpu.SemaphoreType.DMA((8,)),
            pltpu.SemaphoreType.DMA((12,)),
        ],
        compiler_params=params(),
    )(grad_values, rest, w_value, w_query, w_key)
    return (field_grad.reshape(ZL, YL, X, C), value_grad, out_grad, query_grad, key_grad)


def solution(mesh):
    placed = (P("gz", "gy", None, None), P("gz", "gy", None, None), P(), P(), P(), P())
    return jax.shard_map(
        local,
        mesh=mesh,
        in_specs=placed,
        out_specs=(P("gz", "gy", None, None), P(), P(), P(), P()),
        check_vma=False,
    )
```

```python
import jax
import jax.numpy as jnp
from jax import lax
from jax.experimental import pallas as pl
from jax.experimental.pallas import tpu as pltpu
from jax.sharding import PartitionSpec as P

BF = jnp.bfloat16
F32 = jnp.float32
MESH = pl.DeviceIdType.MESH
H = 8
D = 16
C = 128
Z, Y, X = 64, 128, 128
ZL, YL = 2, 32
CELLS = ZL * YL
GZ, GY = 32, 4
EPS = 1e-06
NEAR = (8, 16, 16)
HIGH = lax.Precision.HIGHEST
COUNTS = (Y * X, Z * X, Z * Y)
STARTS = (0, Z, Z + Y)
LENGTHS = (Z, Y, X)
POOLED = Z + Y + X
VMEM = pl.BlockSpec(memory_space=pltpu.VMEM)


def params(**more):
    return pltpu.CompilerParams(vmem_limit_bytes=56 * 2**20, **more)


def dot(a, b):
    return jnp.dot(a, b, preferred_element_type=F32)


def dot_nt(a, b, precision=None):
    return lax.dot_general(
        a, b, (((1,), (1,)), ((), ())), preferred_element_type=F32, precision=precision
    )


def dot_tn(a, b, precision=None):
    return lax.dot_general(
        a, b, (((0,), (0,)), ((), ())), preferred_element_type=F32, precision=precision
    )


def head_stack(block):
    head = lax.broadcasted_iota(jnp.int32, block.shape, 1) % C // D
    zero = jnp.zeros((), block.dtype)
    return jnp.concatenate([jnp.where(head == h, block, zero) for h in range(H)], axis=0)


def head_of(shape):
    return lax.broadcasted_iota(jnp.int32, shape, 1) % C // D


def sides(length):
    return 4 if length == Z else 2


def arrange(heads):
    g = sides(heads[0].shape[0])
    return jnp.concatenate([jnp.concatenate(heads[p : p + g], axis=1) for p in range(0, H, g)], axis=0)


def mix(kernel, lines):
    length = lines[0].shape[0]
    g = sides(length)
    block = jnp.concatenate(lines, axis=1)
    head = head_of(block.shape)
    zero = jnp.zeros((), BF)
    deep = jnp.concatenate([jnp.where(head % g == r, block, zero) for r in range(g)], axis=0)
    tall = dot(kernel[...], deep)
    done = tall[:length]
    for p in range(1, H // g):
        done = jnp.where(head // g == p, tall[p * length : (p + 1) * length], done)
    done = done.astype(BF)
    return [done[:, C * t : C * (t + 1)] for t in range(len(lines))]


def pair_up(left, right):
    g = sides(left[0].shape[0])
    left, right = jnp.concatenate(left, axis=1), jnp.concatenate(right, axis=1)
    head = head_of(left.shape)
    zero = jnp.zeros((), BF)
    tall = jnp.concatenate([jnp.where(head // g == p, left, zero) for p in range(H // g)], axis=0)
    wide = jnp.concatenate([jnp.where(head % g == r, right, zero) for r in range(g)], axis=0)
    return dot_nt(tall, wide)


def apart(score, length):
    g = sides(length)
    heads = []
    for h in range(H):
        p, r = h // g, h % g
        heads.append(score[p * length : (p + 1) * length, r * length : (r + 1) * length])
    return jnp.concatenate(heads, axis=0)


def normalise(pooled, axis):
    means = pooled[pl.ds(STARTS[axis], LENGTHS[axis]), :] / COUNTS[axis]
    scale = lax.rsqrt(jnp.mean(means * means, axis=-1, keepdims=True) + EPS)
    return means * scale, scale


def project(normed, weight):
    return jnp.dot(normed, weight, preferred_element_type=F32, precision=HIGH)


def attention(pooled, w_query, w_key, axis, attn, kernel, back):
    length = LENGTHS[axis]
    normed, _ = normalise(pooled, axis)
    queries = project(normed, w_query[axis])
    keys = project(normed, w_key[axis])
    scores = dot_nt(head_stack(queries), keys, HIGH) * (1.0 / D**0.5)
    grown = jnp.exp(scores - jnp.max(scores, axis=-1, keepdims=True))
    soft = grown / jnp.sum(grown, axis=-1, keepdims=True)
    attn[...] = soft
    heads = [soft[h * length : (h + 1) * length] for h in range(H)]
    kernel[...] = arrange(heads).astype(BF)
    back[...] = arrange([head.T for head in heads]).astype(BF)


def pull(pooled, w_query, w_key, axis, attn, score, out, row_q, row_k):
    length = LENGTHS[axis]
    normed, _ = normalise(pooled, axis)
    queries = head_stack(project(normed, w_query[axis]))
    keys = head_stack(project(normed, w_key[axis]))
    soft, grad = attn[...], apart(score[...], length)
    inner = jnp.sum(soft * grad, axis=-1, keepdims=True)
    grad = soft * (grad - inner) * (1.0 / D**0.5)
    heads = [grad[h * length : (h + 1) * length] for h in range(H)]
    out[pl.ds(row_q, length), :] = jnp.dot(
        jnp.concatenate(heads, axis=1), keys, preferred_element_type=F32, precision=HIGH
    )
    out[pl.ds(row_k, length), :] = dot_tn(grad, queries, HIGH)


def settle(pooled, w_query, w_key, axis, total, row_q, row_k, out, out_q, out_k):
    length = LENGTHS[axis]
    normed, scale = normalise(pooled, axis)
    grad_q = total[pl.ds(row_q, length), :]
    grad_k = total[pl.ds(row_k, length), :]
    out[pl.ds(out_q, C), :] = dot_tn(normed, grad_q, HIGH)
    out[pl.ds(out_k, C), :] = dot_tn(normed, grad_k, HIGH)
    grad = dot_nt(grad_q, w_query[axis], HIGH) + dot_nt(grad_k, w_key[axis], HIGH)
    inner = jnp.mean(grad * normed, axis=-1, keepdims=True)
    return scale * (grad - normed * inner) / COUNTS[axis]


def torus():
    gz, gy = lax.axis_index("gz"), lax.axis_index("gy")
    z, y = lax.div(gz, 8), lax.rem(lax.div(gz, 2), 4)
    x, core = lax.div(gy, 2) * 2 + lax.rem(gz, 2), lax.rem(gy, 2)
    lines = [
        [(lax.rem(z + dz, 4) * 4 + lax.rem(y + dy, 4)) * 2 for dy in range(4)] for dz in range(4)
    ]
    return lines, x, core


def shifts(step, first=0):
    lines, x, core = torus()
    to_core = lax.rem(core + lax.div(step, 4), 2)
    turn = x + lax.rem(step, 4)
    sides = []
    for dx in range(4):
        to_x = lax.rem(turn + dx, 4)
        sides.append((lax.rem(to_x, 2), lax.div(to_x, 2) * 2 + to_core))
    found = []
    for j in range(first, 16):
        dz, dy = j % 4, (j // 4 + j) % 4
        low, gy = sides[(j // 4 + 2 * j) % 4]
        found.append((lines[dz][dy] + low, gy))
    return found


def each_device(visit, first, last):
    def step(i, carry):
        for device in shifts(i):
            visit(device)
        return carry

    if first == 0:
        for device in shifts(jnp.int32(0), 1):
            visit(device)
        first = 1
    lax.fori_loop(first, last, step, 0)


def mine():
    return lax.axis_index("gz") * GY + lax.axis_index("gy")


def wait_bytes(ref, sem):
    pltpu.make_async_copy(ref, ref, sem).wait()


def send(src, dst, send_sem, recv_sem, first=0, last=8, part=None):
    me = mine()

    def block(ref, index):
        return ref.at[index] if part is None else ref.at[index, part]

    def visit(device):
        pltpu.make_async_remote_copy(
            block(src, device[0] * GY + device[1]), block(dst, me), send_sem, recv_sem,
            device_id=device, device_id_type=MESH,
        ).start()

    each_device(visit, first, last)


def keep(src, dst):
    me = mine()
    dst[me] = src[me]


def wait_all(ref, sem, part=None):
    if part is None:
        wait_bytes(ref.at[pl.ds(0, 127)], sem)
    else:
        wait_bytes(ref.at[pl.ds(0, 127), part], sem)


class Sum:
    def __init__(self, src, out, near, wide, sems):
        self.src, self.out, self.near, self.wide, self.sems = src, out, near, wide, sems
        self.near_size, self.wide_size = near.shape[0], wide.shape[0]
        self.piece = src.shape[0] // self.near_size
        self.lows = self.near_size // 4
        gz, gy = lax.axis_index("gz"), lax.axis_index("gy")
        self.low, self.gy = lax.rem(gz, self.lows), gy
        self.line, self.side = lax.div(gz, self.lows), self.low * 4 + gy

    def rows(self, index):
        return pl.ds(pl.multiple_of(index * self.piece, 8), self.piece)

    def near_peer(self, k):
        peer = lax.rem(self.side + k, self.near_size)
        return peer, (self.line * self.lows + lax.div(peer, 4), lax.rem(peer, 4))

    def wide_peer(self, k):
        peer = lax.rem(self.line + k, self.wide_size)
        return peer, (peer * self.lows + self.low, self.gy)

    def copy(self, src, dst, first, device):
        pltpu.make_async_remote_copy(
            src, dst, self.sems.at[first], self.sems.at[first + 1], device_id=device, device_id_type=MESH
        ).start()

    def first(self):
        for k in range(1, self.near_size):
            peer, device = self.near_peer(k)
            self.copy(self.src.at[self.rows(peer)], self.near.at[self.side], 0, device)
        self.near[self.side] = self.src[self.rows(self.side)]

    def second(self):
        wait_bytes(self.near.at[pl.ds(0, self.near_size - 1)], self.sems.at[1])
        self.wide[self.line] = jnp.sum(self.near[...], axis=0)
        for k in range(1, self.wide_size):
            peer, device = self.wide_peer(k)
            self.copy(self.wide.at[self.line], self.wide.at[self.line], 2, device)

    def third(self):
        wait_bytes(self.wide.at[pl.ds(0, self.wide_size - 1)], self.sems.at[3])
        rows = self.rows(self.side)
        self.out[rows] = jnp.sum(self.wide[...], axis=0)
        for k in range(1, self.near_size):
            peer, device = self.near_peer(k)
            self.copy(self.out.at[rows], self.out.at[rows], 4, device)

    def end(self):
        wait_bytes(self.near.at[pl.ds(0, self.near_size - 1)], self.sems.at[5])

    def close(self):
        wait_bytes(self.near.at[pl.ds(0, self.near_size - 1)], self.sems.at[0])
        wait_bytes(self.wide.at[pl.ds(0, self.wide_size - 1)], self.sems.at[2])
        wait_bytes(self.near.at[pl.ds(0, self.near_size - 1)], self.sems.at[4])


def whole_kernel(
    fields_in, cot_in, w_value_in, w_out_in, w_query_in, w_key_in,
    grad_values_out, rest_out,
    fields, cot, cot_s, cot_r, cot_y, mixed_y, grad_y, grad_s, after_s, after_r, after_y, grad_r, values, grad_values,
    held, w_value, w_out, w_query, w_key,
    attn_z, kernel_z, back_z, attn_y, kernel_y, back_y, attn_x, kernel_x, back_x,
    score_z, score_y, score_x, early_rest,
    sum0, pooled, near0, wide0, sum1, total1, near1, wide1, sum2, total2, near2, wide2,
    load_sems, store_sems, move_sems, sums0, sums1, sums2, group_in,
):
    gz, gy = lax.axis_index("gz"), lax.axis_index("gy")

    def load(i, src, dst, base):
        return pltpu.make_async_copy(src.at[pl.ds(16 * i, 16)], dst.at[pl.ds(16 * i, 16)], load_sems.at[base + i])

    weights = [
        pltpu.make_async_copy(src, dst, load_sems.at[8 + i])
        for i, (src, dst) in enumerate(
            ((w_value_in, w_value), (w_out_in, w_out), (w_query_in, w_query), (w_key_in, w_key))
        )
    ]
    for i in range(4):
        load(i, fields_in, fields, 0).start()
    for i in range(4):
        load(i, cot_in, cot, 4).start()
    for copy in weights:
        copy.start()

    means = Sum(sum0, pooled, near0, wide0, sums0)
    barrier = pltpu.get_barrier_semaphore()
    for k in range(1, 8):
        pl.semaphore_signal(barrier, inc=1, device_id=means.near_peer(k)[1], device_id_type=MESH)
    for k in range(1, 16):
        pl.semaphore_signal(barrier, inc=1, device_id=means.wide_peer(k)[1], device_id_type=MESH)
    other = lax.div(gz, 4) * 4 + 2 - lax.div(lax.rem(gz, 4), 2) * 2
    for k in range(1, 8):
        device = (other + lax.rem(lax.rem(gz, 2) + k // 4, 2), lax.rem(gy + k % 4, 4))
        pl.semaphore_signal(barrier, inc=1, device_id=device, device_id_type=MESH)

    sum0[...] = jnp.zeros_like(sum0)
    for i in range(4):
        load(i, fields_in, fields, 0).wait()
        block = fields[pl.ds(16 * i, 16)].astype(F32)
        cells = jnp.sum(block, axis=1)
        sum0[pl.ds(Z + Y, X), :] += jnp.sum(block, axis=0)
        sum0[pl.ds(gz * ZL + i // 2, 1), :] += jnp.sum(cells, axis=0, keepdims=True)
        sum0[pl.ds(pl.multiple_of(Z + gy * YL + (i % 2) * 16, 16), 16), :] += cells
    for copy in weights:
        copy.wait()

    def project_values(i, carry):
        start = pl.multiple_of(i * 16, 16)
        flat = fields[pl.ds(start, 16)].reshape(16 * X, C)
        values[pl.ds(start, 16)] = dot(flat, w_value[...]).astype(BF).reshape(16, X, C)
        return carry

    lax.fori_loop(0, 4, project_values, 0)
    pl.semaphore_wait(barrier, 29)
    means.first()
    for k in range(1, 16):
        pl.semaphore_signal(group_in, inc=1, device_id=means.wide_peer(k)[1], device_id_type=MESH)
    for i in range(4):
        load(i, cot_in, cot, 4).wait()
        cot_s[:, pl.ds(16 * i, 16), :] = jnp.swapaxes(cot[pl.ds(16 * i, 16)], 0, 1)
    pl.semaphore_wait(group_in, 15)
    send(cot_s, cot_r, move_sems.at[0], move_sems.at[1], 0, 1)
    keep(cot_s, cot_r)
    means.second()
    send(cot_s, cot_r, move_sems.at[0], move_sems.at[1], 1, 3)
    means.third()
    send(cot_s, cot_r, move_sems.at[0], move_sems.at[1], 3, 8)

    means.end()

    attention(pooled, w_query, w_key, 2, attn_x, kernel_x, back_x)

    def over_x(i, carry):
        start = pl.multiple_of(i * 16, 16)
        for t in range(0, 16, 8):
            lines = mix(kernel_x, [values[start + t + n] for n in range(8)])
            for n in range(8):
                held[t + n] = lines[n]
        after_s[:, pl.ds(start, 16), :] = jnp.swapaxes(held[...], 0, 1)
        return carry

    lax.fori_loop(0, 4, over_x, 0)
    send(after_s, after_r, move_sems.at[2], move_sems.at[3])
    keep(after_s, after_r)
    attention(pooled, w_query, w_key, 0, attn_z, kernel_z, back_z)
    attention(pooled, w_query, w_key, 1, attn_y, kernel_y, back_y)
    means.close()

    wait_all(cot_r, move_sems.at[1])

    def back_over_z(step, carry):
        side, start = lax.div(step, 2), pl.multiple_of(lax.rem(step, 2) * 16, 16)
        y_start = pl.multiple_of(step * 16, 16)
        lines = []
        for low in range(ZL):
            lines.append(
                jnp.stack(
                    [cot_r[g * GY + side, pl.ds(low * YL + start, 16), :] for g in range(GZ)], axis=0
                )
            )
        block = jnp.stack(lines, axis=1).reshape(Z, 16, C)
        turned = jnp.swapaxes(block, 0, 1)
        cot_y[pl.ds(y_start, 16)] = turned
        grad_mixed = dot_nt(turned.reshape(16 * Z, C), w_out[...]).astype(BF).reshape(16, Z, C)
        mixed_y[pl.ds(y_start, 16)] = grad_mixed
        for t in range(0, 16, 8):
            lines = mix(back_z, [grad_mixed[t + n] for n in range(8)])
            for n in range(8):
                held[t + n, pl.ds(0, Z), :] = lines[n]
        grad_y[:, pl.ds(y_start, 16), :] = jnp.swapaxes(held[:, pl.ds(0, Z), :], 0, 1)
        return carry

    lax.fori_loop(0, 8, back_over_z, 0)

    def back_over_y(step, carry):
        lines = mix(back_y, [grad_y[step * 8 + n] for n in range(8)])
        for n in range(8):
            for side in range(GY):
                grad_s[(step * 4 + n // 2) * GY + side, pl.ds(n % 2 * YL, YL), :] = lines[n][
                    side * YL : (side + 1) * YL
                ]
        return carry

    lax.fori_loop(0, Z // 8, back_over_y, 0)
    halves = (pl.ds(0, YL), pl.ds(YL, YL))
    for low in range(ZL):
        send(grad_s, grad_r, move_sems.at[4], move_sems.at[5 + low], part=halves[low])
    keep(grad_s, grad_r)

    score_z[...] = jnp.zeros_like(score_z)
    score_y[...] = jnp.zeros_like(score_y)
    sum1[pl.ds(2 * (Z + Y), C), :] = jnp.zeros((C, C), F32)
    wait_all(after_r, move_sems.at[3])

    def over_y(step, carry):
        lines = []
        for n in range(8):
            lines.append(
                jnp.concatenate(
                    [after_r[(step * 4 + n // 2) * GY + side, pl.ds(n % 2 * YL, YL), :] for side in range(GY)], axis=0
                )
            )
        done = mix(kernel_y, lines)
        for n in range(8):
            after_y[step * 8 + n] = done[n]
        score_y[...] += pair_up([grad_y[step * 8 + n] for n in range(8)], lines)
        return carry

    lax.fori_loop(0, Z // 8, over_y, 0)

    def over_z(step, carry):
        y_start = pl.multiple_of(step * 16, 16)
        lines = jnp.swapaxes(after_y[:, pl.ds(y_start, 16), :], 0, 1)
        grad_mixed = mixed_y[pl.ds(y_start, 16)]
        parts = []
        for t in range(0, 16, 8):
            group = [lines[t + n] for n in range(8)]
            parts += mix(kernel_z, group)
            score_z[...] += pair_up([grad_mixed[t + n] for n in range(8)], group)
        mixed = jnp.concatenate(parts, axis=0)
        sum1[pl.ds(2 * (Z + Y), C), :] += dot_tn(mixed, cot_y[pl.ds(y_start, 16)].reshape(16 * Z, C))
        return carry

    lax.fori_loop(0, 8, over_z, 0)
    pull(pooled, w_query, w_key, 0, attn_z, score_z, sum1, 0, Z)
    pull(pooled, w_query, w_key, 1, attn_y, score_y, sum1, 2 * Z, 2 * Z + Y)
    early = Sum(sum1, total1, near1, wide1, sums1)
    early.first()

    score_x[...] = jnp.zeros_like(score_x)
    sum2[pl.ds(2 * X, C), :] = jnp.zeros((C, C), F32)

    def home(i, carry):
        start = pl.multiple_of(i * 16, 16)
        grad_x = jnp.swapaxes(grad_r[:, pl.ds(start, 16), :], 0, 1)
        for t in range(0, 16, 8):
            group = [grad_x[t + n] for n in range(8)]
            lines = mix(back_x, group)
            for n in range(8):
                grad_values[start + t + n] = lines[n]
            score_x[...] += pair_up(group, [values[start + t + n] for n in range(8)])
        grad = grad_values[pl.ds(start, 16)].reshape(16 * X, C)
        sum2[pl.ds(2 * X, C), :] += dot_tn(fields[pl.ds(start, 16)].reshape(16 * X, C), grad)
        return carry

    wait_all(grad_r, move_sems.at[5], halves[0])
    lax.fori_loop(0, 2, home, 0)
    wait_all(grad_r, move_sems.at[6], halves[1])
    lax.fori_loop(2, 4, home, 0)
    early.second()
    pull(pooled, w_query, w_key, 2, attn_x, score_x, sum2, 0, X)
    late = Sum(sum2, total2, near2, wide2, sums2)
    late.first()
    store_values = pltpu.make_async_copy(grad_values, grad_values_out, store_sems.at[0])
    store_values.start()
    late.second()
    early.third()
    late.third()
    early.end()
    early_rest[pl.ds(0, C), :] = total1[pl.ds(2 * (Z + Y), C), :]
    early_rest[pl.ds(5 * C, X), :] = pooled[pl.ds(Z + Y, X), :]
    early_rest[pl.ds(6 * C, Z), :] = settle(pooled, w_query, w_key, 0, total1, 0, Z, early_rest, C, 3 * C)
    early_rest[pl.ds(6 * C + Z, Y), :] = settle(
        pooled, w_query, w_key, 1, total1, 2 * Z, 2 * Z + Y, early_rest, 2 * C, 4 * C
    )
    store_early = pltpu.make_async_copy(early_rest, rest_out.at[pl.ds(3 * C, 7 * C + Z)], store_sems.at[1])
    store_early.start()
    late.end()
    store_late = pltpu.make_async_copy(total2, rest_out.at[pl.ds(0, 3 * C)], store_sems.at[2])
    store_late.start()
    wait_all(cot_s, move_sems.at[0])
    wait_all(after_s, move_sems.at[2])
    wait_all(grad_s, move_sems.at[4])
    early.close()
    late.close()
    store_values.wait()
    store_early.wait()
    store_late.wait()


REST = 10 * C + Z


def finish_kernel(
    grad_values_in, rest_in, w_value_in, w_query_in, w_key_in,
    field_grad, value_grad, out_grad, query_grad, key_grad,
    grad_values, rest, w_value, w_query, w_key, query_x, key_x, done, load_sems, store_sems,
):
    gz, gy = lax.axis_index("gz"), lax.axis_index("gy")
    loads = [
        pltpu.make_async_copy(rest_in, rest, load_sems.at[4]),
        pltpu.make_async_copy(w_query_in.at[pl.ds(2, 1)], w_query, load_sems.at[5]),
        pltpu.make_async_copy(w_key_in.at[pl.ds(2, 1)], w_key, load_sems.at[6]),
        pltpu.make_async_copy(w_value_in, w_value, load_sems.at[7]),
    ]

    def part(src, dst, i, sem):
        return pltpu.make_async_copy(src.at[pl.ds(16 * i, 16)], dst.at[pl.ds(16 * i, 16)], sem)

    for copy in loads:
        copy.start()
    for i in range(4):
        part(grad_values_in, grad_values, i, load_sems.at[i]).start()
    for copy in loads:
        copy.wait()

    def block(i):
        return rest.at[pl.ds(C * i, C)]

    stores = [
        pltpu.make_async_copy(block(2), value_grad, store_sems.at[4]),
        pltpu.make_async_copy(block(3), out_grad, store_sems.at[5]),
        pltpu.make_async_copy(block(4), query_grad.at[0], store_sems.at[6]),
        pltpu.make_async_copy(block(5), query_grad.at[1], store_sems.at[7]),
        pltpu.make_async_copy(block(6), key_grad.at[0], store_sems.at[8]),
        pltpu.make_async_copy(block(7), key_grad.at[1], store_sems.at[9]),
        pltpu.make_async_copy(query_x, query_grad.at[2], store_sems.at[10]),
        pltpu.make_async_copy(key_x, key_grad.at[2], store_sems.at[11]),
    ]
    for copy in stores[:6]:
        copy.start()
    means = rest[pl.ds(8 * C, X), :] / COUNTS[2]
    scale = lax.rsqrt(jnp.mean(means * means, axis=-1, keepdims=True) + EPS)
    normed = means * scale
    grad_q, grad_k = rest[pl.ds(0, X), :], rest[pl.ds(X, X), :]
    query_x[...] = dot_tn(normed, grad_q, HIGH)
    key_x[...] = dot_tn(normed, grad_k, HIGH)
    for copy in stores[6:]:
        copy.start()
    grad = dot_nt(grad_q, w_query[0], HIGH) + dot_nt(grad_k, w_key[0], HIGH)
    inner = jnp.mean(grad * normed, axis=-1, keepdims=True)
    means_x = scale * (grad - normed * inner) / COUNTS[2]
    for i in range(4):
        part(grad_values_in, grad_values, i, load_sems.at[i]).wait()
        direct = dot_nt(grad_values[pl.ds(16 * i, 16)].reshape(16 * X, C), w_value[...]).reshape(16, X, C)
        part_z = rest[pl.ds(9 * C + gz * ZL + i // 2, 1), :]
        part_y = rest[pl.ds(pl.multiple_of(9 * C + Z + gy * YL + (i % 2) * 16, 16), 16), :]
        cells = part_z + part_y
        done[pl.ds(16 * i, 16)] = (direct + cells[:, None, :] + means_x[None]).astype(BF)
        part(done, field_grad, i, store_sems.at[i]).start()
    for i in range(4):
        part(done, field_grad, i, store_sems.at[i]).wait()
    for copy in stores:
        copy.wait()


def local(fields, cotangent, w_value, w_out, w_query, w_key):
    hbm = pl.BlockSpec(memory_space=pltpu.HBM)
    cells = (CELLS, X, C)
    blocks = (X, CELLS, C)
    sums = []
    for rows, near in zip((POOLED, 2 * (Z + Y) + C, 2 * X + C), NEAR):
        sums += [
            pltpu.VMEM((rows, C), F32),
            pltpu.VMEM((rows, C), F32),
            pltpu.VMEM((near, rows // near, C), F32),
            pltpu.VMEM((128 // near, rows // near, C), F32),
        ]
    map_shapes = []
    for length in LENGTHS:
        map_shapes += [
            pltpu.VMEM((H * length, length), F32),
            pltpu.VMEM((H // sides(length) * length, sides(length) * length), BF),
            pltpu.VMEM((H // sides(length) * length, sides(length) * length), BF),
        ]
    field_shapes = [
        cells, cells, blocks, blocks, (Y, Z, C), (Y, Z, C), (Z, Y, C), blocks, blocks, blocks, (Z, Y, C), blocks,
        cells, cells,
    ]
    weights = [pltpu.VMEM((C, C), BF)] * 2 + [pltpu.VMEM((3, C, C), F32)] * 2
    grad_values, rest = pl.pallas_call(
        whole_kernel,
        in_specs=[hbm] * 6,
        out_specs=[hbm] * 2,
        out_shape=[jax.ShapeDtypeStruct(cells, BF), jax.ShapeDtypeStruct((REST, C), F32)],
        scratch_shapes=[pltpu.VMEM(shape, BF) for shape in field_shapes]
        + [pltpu.VMEM((16, X, C), BF)]
        + weights
        + map_shapes
        + [
            pltpu.VMEM((H // sides(Z) * Z, sides(Z) * Z), F32),
            pltpu.VMEM((H // sides(Y) * Y, sides(Y) * Y), F32),
            pltpu.VMEM((H // sides(X) * X, sides(X) * X), F32),
            pltpu.VMEM((7 * C + Z, C), F32),
        ]
        + sums
        + [pltpu.SemaphoreType.DMA((count,)) for count in (12, 3, 7, 6, 6, 6)]
        + [pltpu.SemaphoreType.REGULAR],
        compiler_params=params(collective_id=0, has_side_effects=True),
    )(fields.reshape(cells), cotangent.reshape(cells), w_value, w_out, w_query, w_key)
    square = jax.ShapeDtypeStruct((C, C), F32)
    cube = jax.ShapeDtypeStruct((3, C, C), F32)
    field_grad, value_grad, out_grad, query_grad, key_grad = pl.pallas_call(
        finish_kernel,
        in_specs=[hbm] * 5,
        out_specs=[hbm] * 5,
        out_shape=[jax.ShapeDtypeStruct(cells, BF), square, square, cube, cube],
        scratch_shapes=[
            pltpu.VMEM(cells, BF),
            pltpu.VMEM((REST, C), F32),
            pltpu.VMEM((C, C), BF),
            pltpu.VMEM((1, C, C), F32),
            pltpu.VMEM((1, C, C), F32),
            pltpu.VMEM((C, C), F32),
            pltpu.VMEM((C, C), F32),
            pltpu.VMEM(cells, BF),
            pltpu.SemaphoreType.DMA((8,)),
            pltpu.SemaphoreType.DMA((12,)),
        ],
        compiler_params=params(),
    )(grad_values, rest, w_value, w_query, w_key)
    return (field_grad.reshape(ZL, YL, X, C), value_grad, out_grad, query_grad, key_grad)


def solution(mesh):
    placed = (P("gz", "gy", None, None), P("gz", "gy", None, None), P(), P(), P(), P())
    return jax.shard_map(
        local,
        mesh=mesh,
        in_specs=placed,
        out_specs=(P("gz", "gy", None, None), P(), P(), P(), P()),
        check_vma=False,
    )
```
